512 devices in a mesh: gx: 4 (over y), gy: 4 (over x), gz: 32 (over z, core).
Axes of the slice: x: 4, y: 4, z: 16, core: 2. Of those that a mesh axis runs over, the one named last changes fastest.
Arguments:
- seg_offset: float32 [3, 16, 4, 32, 256], P(None, 'gx', 'gy', 'gz'), may hold values from 0 to 1
- seg_vector: float32 [3, 16, 4, 32, 256], P(None, 'gx', 'gy', 'gz'), may hold values from -1.8 to 1.8
- burgers: float32 [3, 16, 4, 32, 256], P(None, 'gx', 'gy', 'gz'), may hold values from -6 to 6
- cell_counts: int32 [16, 4, 32], P('gx', 'gy', 'gz'), may hold values from 1 to 256, as said below
- applied: float32 [3, 3], replicated, may hold values from -4 to 4
Outputs:
- forces: float32 [3, 16, 4, 32, 256], P(None, 'gx', 'gy', 'gz')
The draws below stay inside these ranges and needn't reach their ends.
Inputs may be any that keep to these rules, and one draw needn't show every extreme that they name: `cell_counts`: A cell's live segments fill its first slots; some cell is full.
All inputs are finite; a program needn't handle non-finite values.
Results may differ from the reference program's by a relative error of at most 0.0003.
Values sent between devices are 32-bit elements; how exact they have to be, the bound alone decides.
No kernel may reach another device: no remote copies, remote signals or barrier semaphores. Data moves between devices by JAX's collectives and lax.ppermute only.
A program may use at most 64 MiB of HBM per device.

```python
import math
import jax
import jax.numpy as jnp
import numpy as np
from jax import lax

CAP = 256
NX = 16
NY = 4
NZ = 32


def draw_cell_counts(key, part):
    key = jax.random.fold_in(key, 7)
    level_key, base_key, spot_key = jax.random.split(key, 3)
    levels = jax.random.randint(level_key, (NZ,), 1, 9)
    base = jax.random.randint(base_key, (NX, NY, NZ), 0, CAP)
    counts = 1 + base * levels[None, None, :] // 8
    spot_x = jax.random.randint(jax.random.fold_in(spot_key, 1), (), 0, NX)
    spot_y = jax.random.randint(jax.random.fold_in(spot_key, 2), (), 0, NY)
    spot_z = jax.random.randint(jax.random.fold_in(spot_key, 3), (), 0, NZ)
    counts = counts.at[spot_x, spot_y, spot_z].set(CAP)
    return counts.astype(jnp.int32)


def shard_levels(key, shape, cuts, smallest, top_value):
    factor_of = 1.0
    for position, blocks in cuts:
        draws = jax.random.uniform(jax.random.fold_in(jax.random.fold_in(key, 6), position), (blocks,), jnp.float32, smallest / len(cuts), top_value / len(cuts))
        factor_of = factor_of * jnp.repeat(jnp.exp(draws), shape[position] // blocks).reshape((-1,) + (1,) * (len(shape) - 1 - position))
    return factor_of


def scatter_about(own_key, extent, width, reach, shards=(), kind=jnp.bfloat16):
    factor_of = shard_levels(own_key, extent, shards, -0.22, 0.18) if shards else 1.0
    values = jax.random.normal(own_key, extent, jnp.float32) * width * factor_of
    return jnp.minimum(jnp.maximum(values, -reach), reach).astype(kind)


def setup_inputs(seed: int = 0) -> dict:
    key_of = jax.random.split(jax.random.key(seed), 6)
    return {
        "seg_offset": jnp.clip(1.0 * jax.random.uniform(key_of[0], (3, NX, NY, NZ, CAP), jnp.float32) ** shard_levels(key_of[0], (3, NX, NY, NZ, CAP), ((1, 4), (2, 4), (3, 32)), -0.2, 0.2), 0.0, 1.0),
        "seg_vector": scatter_about(key_of[1], (3, NX, NY, NZ, CAP), 0.3, 1.8, ((1, 4), (2, 4), (3, 32)), jnp.float32),
        "burgers": scatter_about(key_of[2], (3, NX, NY, NZ, CAP), 1.0, 6.0, ((1, 4), (2, 4), (3, 32)), jnp.float32),
        "cell_counts": draw_cell_counts(jax.random.fold_in(key_of[5], 71), 0),
        "applied": scatter_about(key_of[4], (3, 3), 1.0, 4.0, (), jnp.float32),
    }


CORE_WIDTH = 0.2
FIRST_COEF = 1.0 / (8.0 * math.pi)
SECOND_COEF = 1.0 / (4.0 * math.pi * 0.7)
NEIGHBOURS = np.array([[step_x, step_y, step_z] for step_x in (-1, 0, 1) for step_y in (-1, 0, 1) for step_z in (-1, 0, 1)], dtype=np.int32)

def dotted(left_vec, right_vec):
    return left_vec[0] * right_vec[0] + left_vec[1] * right_vec[1] + left_vec[2] * right_vec[2]

def crossed(left_vec, right_vec):
    return (left_vec[1] * right_vec[2] - left_vec[2] * right_vec[1], left_vec[2] * right_vec[0] - left_vec[0] * right_vec[2], left_vec[0] * right_vec[1] - left_vec[1] * right_vec[0])

def factors(apart):
    square = dotted(apart, apart) + CORE_WIDTH * CORE_WIDTH
    inverse = lax.rsqrt(square)
    recip_cube = inverse * inverse * inverse
    recip_fifth = recip_cube * inverse * inverse
    radial = 2.0 * recip_cube + 3.0 * CORE_WIDTH * CORE_WIDTH * recip_fifth
    return (recip_cube, recip_fifth, radial)

def pair_sum(apart, tangent, burgers_src, wedges, target, axis_sum):
    recip_cube, recip_fifth, radial = factors(apart)
    turned = crossed(apart, burgers_src)
    tangent_dot = dotted(tangent, target)
    turned_dot = dotted(turned, target)
    wedge_dot = dotted(wedges, target)
    apart_dot = dotted(apart, target)
    wedge_apart = dotted(wedges, apart)
    first_part = wedge_apart * (radial - recip_cube)
    third_part = 3.0 * wedge_apart * apart_dot * recip_fifth
    pieces = []
    for which in range(3):
        summand = -FIRST_COEF * radial * (turned[which] * tangent_dot + tangent[which] * turned_dot) + SECOND_COEF * (target[which] * first_part - (wedges[which] * apart_dot + apart[which] * wedge_dot) * recip_cube + apart[which] * third_part)
        pieces.append(lax.optimization_barrier(jnp.sum(summand, axis=axis_sum)))
    return jnp.stack(pieces)

def distant_sum(apart, moment, distant):
    recip_cube, recip_fifth, radial = factors(apart)
    wedges = (moment[5] - moment[7], moment[6] - moment[2], moment[1] - moment[3])
    wedge_apart = dotted(wedges, apart)
    turned = [crossed(apart, (moment[column], moment[3 + column], moment[6 + column])) for column in range(3)]
    pieces = []
    for row_axis in range(3):
        for col_axis in range(3):
            element = -FIRST_COEF * radial * (turned[col_axis][row_axis] + turned[row_axis][col_axis]) + SECOND_COEF * (3.0 * wedge_apart * apart[row_axis] * apart[col_axis] * recip_fifth - (wedges[row_axis] * apart[col_axis] + wedges[col_axis] * apart[row_axis]) * recip_cube)
            if row_axis == col_axis:
                element = element + SECOND_COEF * wedge_apart * (radial - recip_cube)
            pieces.append(lax.optimization_barrier(jnp.sum(jnp.where(distant, element, 0.0), axis=-1)))
    return jnp.stack(pieces)

def reference(seg_offset, seg_vector, burgers, cell_counts, applied):
    slot_ids = jnp.arange(CAP, dtype=jnp.int32)
    filled = slot_ids[None, None, None, :] < cell_counts[..., None]
    tangent_live = jnp.where(filled[None], seg_vector, 0.0)
    burgers_live = jnp.where(filled[None], burgers, 0.0)
    wedges = jnp.stack(crossed(burgers_live, tangent_live))
    packed = jnp.concatenate([seg_offset, tangent_live, burgers_live, wedges])
    padded = jnp.pad(packed, ((0, 0), (1, 1), (1, 1), (1, 1), (0, 0)))
    displace = jnp.asarray(NEIGHBOURS.T).astype(jnp.float32)
    anchor = jnp.zeros((), jnp.int32)

    def one_cell(cell_index):
        coord_x = (cell_index // (NY * NZ)).astype(jnp.int32)
        coord_y = (cell_index // NZ % NY).astype(jnp.int32)
        coord_z = (cell_index % NZ).astype(jnp.int32)
        source_block = lax.dynamic_slice(padded, (anchor, coord_x, coord_y, coord_z, anchor), (12, 3, 3, 3, CAP)).reshape(12, 27, CAP)
        owned = lax.dynamic_slice(packed, (anchor, coord_x, coord_y, coord_z, anchor), (12, 1, 1, 1, CAP)).reshape(12, CAP)
        apart = owned[0:3, None, :, None] - source_block[0:3, :, None, :] - displace[:, :, None, None]
        return pair_sum(apart, source_block[3:6, :, None, :], source_block[6:9, :, None, :], source_block[9:12, :, None, :], owned[6:9, None, :, None], (0, 2))
    nearby = lax.map(one_cell, jnp.arange(NX * NY * NZ, dtype=jnp.int32))
    nearby = jnp.moveaxis(nearby, 1, 0).reshape(3, NX, NY, NZ, CAP)
    cell_ids = jnp.arange(NX * NY * NZ, dtype=jnp.int32)
    coords = jnp.stack([cell_ids // (NY * NZ), cell_ids // NZ % NY, cell_ids % NZ]).astype(jnp.float32)
    apart = coords[:, :, None] - coords[:, None, :]
    distant = lax.optimization_barrier(jnp.max(jnp.abs(apart), axis=0)) > 1.5
    moment = lax.optimization_barrier(jnp.sum(burgers_live[:, None] * tangent_live[None, :], axis=-1)).reshape(9, NX * NY * NZ)
    distant_stress = distant_sum(apart, moment[:, None, :], distant).reshape(9, NX, NY, NZ)
    symmetric = 0.5 * (applied + applied.T)
    stress = distant_stress + symmetric.reshape(9)[:, None, None, None]
    rows = []
    for row_axis in range(3):
        rows.append(stress[row_axis * 3][..., None] * burgers_live[0] + stress[row_axis * 3 + 1][..., None] * burgers_live[1] + stress[row_axis * 3 + 2][..., None] * burgers_live[2])
    total = nearby + jnp.stack(rows)
    return jnp.stack(crossed(total, tangent_live))
```

```python
import functools
import math

import jax
import jax.numpy as jnp
from jax import lax
from jax.experimental import pallas as pl
from jax.experimental.pallas import tpu as pltpu
from jax.sharding import PartitionSpec as P

CORE_SQUARE = 0.2 * 0.2
FIRST = 1.0 / (8.0 * math.pi)
SECOND = 1.0 / (4.0 * math.pi * 0.7)
KAPPA = 3.0 * CORE_SQUARE
CAP = 256
LANES = 128
ROWS = 10
PAIRS = ((0, 0), (0, 1), (0, 2), (1, 1), (1, 2), (2, 2))
NUM3 = 32
NUM5 = 48


def cross(a, b):
    return (
        a[1] * b[2] - a[2] * b[1],
        a[2] * b[0] - a[0] * b[2],
        a[0] * b[1] - a[1] * b[0],
    )


def plus(terms):
    terms = [t for t in terms if t is not None]
    total = terms[0]
    for t in terms[1:]:
        total = total + t
    return total


def features(y, t, b):
    w = cross(b, t)
    turn = [[None, b[2], -b[1]], [-b[2], None, b[0]], [b[1], -b[0], None]]
    c2w = [SECOND * v for v in w]
    lin3, lin5 = {}, {}
    for n, (i, j) in enumerate(PAIRS):
        for m in range(3):
            parts = []
            if turn[i][m] is not None:
                parts.append(turn[i][m] * t[j])
            if turn[j][m] is not None:
                parts.append(turn[j][m] * t[i])
            base = plus(parts) * (-FIRST) if parts else None
            a3 = [2.0 * base] if base is not None else []
            a5 = [base] if base is not None else []
            if i == j:
                a3.append(c2w[m])
                a5.append(c2w[m])
            if m == j:
                a3.append(-c2w[i])
            if m == i:
                a3.append(-c2w[j])
            lin3[m, n] = plus(a3) if a3 else None
            lin5[m, n] = KAPPA * plus(a5) if a5 else None
    w3 = [3.0 * v for v in c2w]
    wy = [[w3[m] * y[n] for n in range(3)] for m in range(3)]
    dot = wy[0][0] + wy[1][1] + wy[2][2]
    doty = [dot * y[n] for n in range(3)]
    rows3, rows5 = {}, {}
    for n, (i, j) in enumerate(PAIRS):
        zero3, zero5 = [], [doty[i] * y[j]]
        for m in range(3):
            if lin3[m, n] is not None:
                rows3[8 * m + n] = lin3[m, n]
                zero3.append(lin3[m, n] * y[m])
            quad = [wy[m][i] * y[j]]
            if m == i:
                quad.append(doty[j])
            if m == j:
                quad.append(doty[i])
            if lin5[m, n] is not None:
                quad.append(lin5[m, n])
                zero5.append(lin5[m, n] * y[m])
            rows5[8 * m + n] = plus(quad)
        if zero3:
            rows3[24 + n] = -plus(zero3)
        rows5[24 + n] = -plus(zero5)
    for m in range(3):
        for n in range(3):
            rows5[32 + 3 * m + n] = -wy[m][n]
        rows5[41 + m] = w3[m]
    return rows3, rows5


def halves(value, terms):
    out = []
    for k in range(terms):
        part = value.astype(jnp.bfloat16)
        out.append(part)
        if k + 1 < terms:
            value = value - part.astype(jnp.float32)
    return out


def near_kernel(planes, offsets, counts_ref, *refs):
    sources = refs[: len(offsets)]
    refs = refs[len(offsets):]
    own_ref, out_ref = refs[:2]
    raw, feat, wide, left3, left5, live_ref = refs[2:]
    columns = [(k, c, d) for k, group in enumerate(offsets) for c, d in enumerate(group)]
    blocks = -(-(2 * len(columns) + 1) // 8) * 8
    chunks = blocks // 2
    lane = lax.broadcasted_iota(jnp.int32, (ROWS, LANES), 1)
    lift = lax.broadcasted_iota(jnp.int32, (ROWS, LANES), 0)

    raw[...] = jnp.zeros_like(raw)
    feat[...] = jnp.zeros_like(feat)
    out_ref[...] = jnp.zeros_like(out_ref)

    for j in range(planes):
        at = jnp.int32(0)
        for k, c, (dy, dz) in columns:
            cell = c * planes + j
            shift = (
                jnp.where(lift < 3, -0.5, 0.0)
                + jnp.where(lift == 1, float(dy), 0.0)
                + jnp.where(lift == 2, float(dz), 0.0)
            )
            first = sources[k][ROWS * cell: ROWS * cell + ROWS, 0:LANES] + shift
            second = sources[k][ROWS * cell: ROWS * cell + ROWS, LANES:] + shift
            low = jnp.bitwise_and(at, LANES - 1)
            base = lax.shift_right_logical(at, 7) + j * blocks
            first = pltpu.roll(first, low, 1)
            second = pltpu.roll(second, low, 1)
            keep = lane >= low
            place = pl.multiple_of(base * 16, 16)
            raw[pl.ds(place, ROWS), :] = jnp.where(keep, first, raw[pl.ds(place, ROWS), :])
            raw[pl.ds(place + 16, ROWS), :] = jnp.where(keep, second, first)
            raw[pl.ds(place + 32, ROWS), :] = jnp.where(keep, 0.0, second)
            at = at + counts_ref[k * len(offsets[k]) * planes + cell]
        live_ref[j] = at

    def plane_body(j, carry):
        live = live_ref[j]
        groups = lax.shift_right_logical(live + 8 * LANES - 1, 10)
        steps = lax.shift_right_logical(live + CAP - 1, 8)

        def group_body(g, carry):
            start = pl.multiple_of((j * blocks + g * 8) * 16, 128)
            row = [raw[pl.ds(start + r, 8, stride=16), :] for r in range(9)]
            rows3, rows5 = features(row[0:3], row[3:6], row[6:9])
            for r, value in rows3.items():
                feat[pl.ds(r, 8, stride=NUM3 + NUM5), :] = value
            for r, value in rows5.items():
                feat[pl.ds(NUM3 + r, 8, stride=NUM3 + NUM5), :] = value
            for q in range(8):
                piece = halves(feat[q * 80: q * 80 + NUM3, :], 3)
                span = slice((q % 2) * LANES, (q % 2 + 1) * LANES)
                for n in range(3):
                    left3[g * 4 + q // 2, n * NUM3: (n + 1) * NUM3, span] = piece[n]
                piece = halves(feat[q * 80 + NUM3: (q + 1) * 80, :], 3)
                for n in range(3):
                    left5[g * 4 + q // 2, n * NUM5: (n + 1) * NUM5, span] = piece[n]
                turned = jnp.transpose(raw[pl.ds(start + q * 16, 8), :])
                for n in range(3):
                    wide[g * 4 + q // 2, n, (q % 2) * LANES: (q % 2 + 1) * LANES, :] = (
                        jnp.broadcast_to(turned[:, n: n + 1], (LANES, LANES))
                    )
            return carry

        lax.fori_loop(0, groups, group_body, 0)

        def cell_body(i, carry):
            where_x = (i + 1 - j).astype(jnp.float32) - 0.5
            points = [
                own_ref[i, 0:1, :] + where_x,
                own_ref[i, 1:2, :] - 0.5,
                own_ref[i, 2:3, :] - 0.5,
            ]
            targets = counts_ref[counts_ref.shape[0] - 4 + i]

            def run(parts):
                width = parts * LANES
                seen = [
                    [jnp.broadcast_to(v[:, h * LANES:(h + 1) * LANES], (16, LANES)) for v in points]
                    for h in range(parts)
                ]

                def step(c, acc):
                    acc3, acc5 = acc
                    high3, low3, high5, low5 = [], [], [], []
                    for s in range(CAP // 16):
                        there = [wide[c, n, s * 16: (s + 1) * 16, :] for n in range(3)]
                        got = [[], [], [], []]
                        for h in range(parts):
                            d = [seen[h][n] - there[n] for n in range(3)]
                            inv = lax.rsqrt(d[0] * d[0] + d[1] * d[1] + (d[2] * d[2] + CORE_SQUARE))
                            square = inv * inv
                            cube = square * inv
                            fifth = cube * square
                            a, b = halves(cube, 2)
                            e, f = halves(fifth, 2)
                            for store, value in zip(got, (a, b, e, f)):
                                store.append(value)
                        for store, value in zip((high3, low3, high5, low5), got):
                            store.append(jnp.concatenate(value, axis=1) if parts > 1 else value[0])
                    high3, low3, high5, low5 = [
                        jnp.concatenate(v, axis=0) for v in (high3, low3, high5, low5)
                    ]
                    mm = functools.partial(jnp.dot, preferred_element_type=jnp.float32)
                    a = mm(left3[c], high3)
                    b = mm(left3[c, 0:2 * NUM3, :], low3)
                    acc3 = acc3 + (
                        a[0:NUM3]
                        + (a[NUM3:2 * NUM3] + b[0:NUM3])
                        + (a[2 * NUM3:] + b[NUM3:])
                    )
                    a = mm(left5[c], high5)
                    b = mm(left5[c, 0:2 * NUM5, :], low5)
                    acc5 = acc5 + (
                        a[0:NUM5]
                        + (a[NUM5:2 * NUM5] + b[0:NUM5])
                        + (a[2 * NUM5:] + b[NUM5:])
                    )
                    return acc3, acc5

                acc3, acc5 = lax.fori_loop(
                    0,
                    steps,
                    step,
                    (jnp.zeros((NUM3, width), jnp.float32), jnp.zeros((NUM5, width), jnp.float32)),
                )
                x = [v[:, 0:width] for v in points]
                both = acc3 + acc5[0:NUM3]
                linear = both[24:32] + x[0] * both[0:8] + x[1] * both[8:16] + x[2] * both[16:24]
                second = acc5[32:48]
                v = [
                    x[0] * second[n: n + 1] + x[1] * second[3 + n: 4 + n] + x[2] * second[6 + n: 7 + n]
                    for n in range(3)
                ]
                scale = 0.5 * (
                    second[0:1] + second[4:5] + second[8:9]
                    + x[0] * second[9:10] + x[1] * second[10:11] + x[2] * second[11:12]
                )
                v = [v[n] + scale * x[n] for n in range(3)]
                for n, (a, b) in enumerate(PAIRS):
                    out_ref[i, n: n + 1, 0:width] += linear[n: n + 1] + x[a] * v[b] + x[b] * v[a]

            @pl.when(targets > LANES)
            def _():
                run(2)

            @pl.when(targets <= LANES)
            def _():
                run(1)

            return carry

        lax.fori_loop(jnp.maximum(j - 2, 0), jnp.minimum(j + 1, planes - 2), cell_body, 0)
        return carry

    lax.fori_loop(0, planes, plane_body, 0)


def near(planes, offsets, counts, sources, own):
    columns = sum(len(group) for group in offsets)
    blocks = -(-(2 * columns + 1) // 8) * 8
    cells = planes - 2
    vmem = pl.BlockSpec(memory_space=pltpu.VMEM)
    return pl.pallas_call(
        functools.partial(near_kernel, planes, offsets),
        out_shape=jax.ShapeDtypeStruct((cells, 8, CAP), jnp.float32),
        in_specs=[pl.BlockSpec(memory_space=pltpu.SMEM)] + [vmem] * (len(sources) + 1),
        out_specs=vmem,
        scratch_shapes=[
            pltpu.VMEM((planes * blocks * 16, LANES), jnp.float32),
            pltpu.VMEM((8 * (NUM3 + NUM5), LANES), jnp.float32),
            pltpu.VMEM((blocks // 2, 3, CAP, LANES), jnp.float32),
            pltpu.VMEM((blocks // 2, 3 * NUM3, CAP), jnp.bfloat16),
            pltpu.VMEM((blocks // 2, 3 * NUM5, CAP), jnp.bfloat16),
            pltpu.SMEM((planes,), jnp.int32),
        ],
        compiler_params=pltpu.CompilerParams(vmem_limit_bytes=32 * 1024 * 1024),
        name="near_%d" % columns,
    )(counts, *sources, own)


def far_kernel(spans, moment_ref, place_ref, applied_ref, own_ref, *refs):
    parts, out_ref = refs[:-1], refs[-1]
    span_y, span_z = spans
    cells = own_ref.shape[0]
    count = moment_ref.shape[0]
    turned = jnp.transpose(moment_ref[...])
    moment = [turned[cells * m: cells * m + cells, :] for m in range(9)]
    device = lax.broadcasted_iota(jnp.int32, (cells, count), 1)
    inner = lax.broadcasted_iota(jnp.int32, (cells, count), 0)
    source = (
        (device // (span_y * span_z) * cells + inner).astype(jnp.float32),
        (device // span_z % span_y).astype(jnp.float32),
        (device % span_z).astype(jnp.float32),
    )
    w = (moment[5] - moment[7], moment[6] - moment[2], moment[1] - moment[3])
    index = {}
    for n, (a, b) in enumerate(PAIRS):
        index[a, b] = index[b, a] = n
    for i in range(cells):
        mine = (place_ref[0] * cells + i, place_ref[1], place_ref[2])
        r = [mine[n].astype(jnp.float32) - source[n] for n in range(3)]
        reach = jnp.maximum(jnp.maximum(jnp.abs(r[0]), jnp.abs(r[1])), jnp.abs(r[2]))
        inv = lax.rsqrt(r[0] * r[0] + r[1] * r[1] + r[2] * r[2] + CORE_SQUARE)
        inv = jnp.where(reach > 1.5, inv, 0.0)
        cube = inv * inv * inv
        fifth = cube * inv * inv
        radial = 2.0 * cube + KAPPA * fifth
        along = w[0] * r[0] + w[1] * r[1] + w[2] * r[2]
        turn = [cross(r, (moment[n], moment[3 + n], moment[6 + n])) for n in range(3)]
        slope = (3.0 * SECOND) * along * fifth
        cut = SECOND * cube
        bulk = SECOND * along * (radial - cube)
        front = -FIRST * radial
        stress = []
        for n, (a, b) in enumerate(PAIRS):
            element = (
                front * (turn[b][a] + turn[a][b])
                + slope * r[a] * r[b]
                - cut * (w[a] * r[b] + w[b] * r[a])
            )
            if a == b:
                element = element + bulk
            stress.append(
                jnp.sum(element, axis=(0, 1), keepdims=True)
                + 0.5 * (applied_ref[a, b] + applied_ref[b, a])
                + plus([part[i, n: n + 1, :] for part in parts])
            )
        t = [own_ref[i, 3 + n: 4 + n, :] for n in range(3)]
        b = [own_ref[i, 6 + n: 7 + n, :] for n in range(3)]
        force = [plus([stress[index[m, n]] * b[n] for n in range(3)]) for m in range(3)]
        for n, value in enumerate(cross(force, t)):
            out_ref[n, i: i + 1, :] = value


def far(spans, moments, place, applied, own, parts):
    cells = own.shape[0]
    vmem = pl.BlockSpec(memory_space=pltpu.VMEM)
    smem = pl.BlockSpec(memory_space=pltpu.SMEM)
    return pl.pallas_call(
        functools.partial(far_kernel, spans),
        out_shape=jax.ShapeDtypeStruct((3, cells, CAP), jnp.float32),
        in_specs=[vmem, smem, smem, vmem] + [vmem] * len(parts),
        out_specs=vmem,
        compiler_params=pltpu.CompilerParams(vmem_limit_bytes=32 * 1024 * 1024),
        name="far",
    )(moments, place, applied, own, *parts)


def beside(first, last, axis):
    devices = lax.axis_size(axis)
    up = [(i, i + 1) for i in range(devices - 1)]
    down = [(i + 1, i) for i in range(devices - 1)]
    return lax.ppermute(last, axis, up), lax.ppermute(first, axis, down)


def local(seg_offset, seg_vector, burgers, cell_counts, applied):
    cells = seg_offset.shape[1]
    planes = cells + 2
    counts = cell_counts.reshape(cells)
    slots = jnp.arange(CAP, dtype=jnp.int32)
    filled = slots[None, :] < counts[:, None]
    offset = seg_offset.reshape(3, cells, CAP)
    tangent = jnp.where(filled[None], seg_vector.reshape(3, cells, CAP), 0.0)
    charge = jnp.where(filled[None], burgers.reshape(3, cells, CAP), 0.0)
    moment = jnp.sum(charge[:, None] * tangent[None, :], axis=-1).reshape(1, 9 * cells)
    moments = gathered(jnp.pad(moment, ((0, 0), (0, LANES - 9 * cells))))
    level = jnp.broadcast_to(counts.astype(jnp.float32)[None, :, None], (1, cells, CAP))
    own = jnp.concatenate([offset, tangent, charge, level]).transpose(1, 0, 2)
    flat = own.reshape(cells * ROWS, CAP)
    before, after = beside(flat[:ROWS], flat[-ROWS:], "gx")
    column = jnp.concatenate([before, flat, after])
    before, after = beside(column, column, "gy")
    sheet = jnp.concatenate([before, column, after])
    before, after = beside(sheet, sheet, "gz")

    def live(array):
        return array.reshape(-1, ROWS, CAP)[:, ROWS - 1, 0].astype(jnp.int32)

    middle = [(dy, 0) for dy in (-1, 0, 1)]
    outer = [[(dy, dz) for dy in (-1, 0, 1)] for dz in (-1, 1)]
    near_a = near(planes, [middle], jnp.concatenate([live(sheet), counts]), [sheet], own)
    near_b = near(
        planes,
        outer,
        jnp.concatenate([live(before), live(after), counts]),
        [before, after],
        own,
    )
    place = jnp.stack([lax.axis_index(a) for a in ("gx", "gy", "gz")]).astype(jnp.int32)
    spans = (lax.axis_size("gy"), lax.axis_size("gz"))
    result = far(spans, moments, place, applied, own, [near_a, near_b])
    return result.reshape(seg_offset.shape)


def gathered(moment):
    wide = jnp.concatenate([moment] * 8, axis=0)
    whole = lax.all_gather(wide, ("gx", "gy", "gz"), axis=0, tiled=True)
    return whole.reshape(-1, 8, LANES)[:, 0, :]


def solution(mesh):
    placed = P(None, "gx", "gy", "gz", None)
    return jax.shard_map(
        local,
        mesh=mesh,
        in_specs=(placed, placed, placed, P("gx", "gy", "gz"), P()),
        out_specs=placed,
        check_vma=False,
    )
```

```python
import functools
import math

import jax
import jax.numpy as jnp
from jax import lax
from jax.experimental import pallas as pl
from jax.experimental.pallas import tpu as pltpu
from jax.sharding import PartitionSpec as P

CORE_SQUARE = 0.2 * 0.2
FIRST = 1.0 / (8.0 * math.pi)
SECOND = 1.0 / (4.0 * math.pi * 0.7)
KAPPA = 3.0 * CORE_SQUARE
CAP = 256
LANES = 128
ROWS = 10
PAIRS = ((0, 0), (0, 1), (0, 2), (1, 1), (1, 2), (2, 2))
NUM3 = 32
NUM5 = 48


def cross(a, b):
    return (
        a[1] * b[2] - a[2] * b[1],
        a[2] * b[0] - a[0] * b[2],
        a[0] * b[1] - a[1] * b[0],
    )


def plus(terms):
    terms = [t for t in terms if t is not None]
    total = terms[0]
    for t in terms[1:]:
        total = total + t
    return total


def features(y, t, b):
    w = cross(b, t)
    turn = [[None, b[2], -b[1]], [-b[2], None, b[0]], [b[1], -b[0], None]]
    c2w = [SECOND * v for v in w]
    lin3, lin5 = {}, {}
    for n, (i, j) in enumerate(PAIRS):
        for m in range(3):
            parts = []
            if turn[i][m] is not None:
                parts.append(turn[i][m] * t[j])
            if turn[j][m] is not None:
                parts.append(turn[j][m] * t[i])
            base = plus(parts) * (-FIRST) if parts else None
            a3 = [2.0 * base] if base is not None else []
            a5 = [base] if base is not None else []
            if i == j:
                a3.append(c2w[m])
                a5.append(c2w[m])
            if m == j:
                a3.append(-c2w[i])
            if m == i:
                a3.append(-c2w[j])
            lin3[m, n] = plus(a3) if a3 else None
            lin5[m, n] = KAPPA * plus(a5) if a5 else None
    w3 = [3.0 * v for v in c2w]
    wy = [[w3[m] * y[n] for n in range(3)] for m in range(3)]
    dot = wy[0][0] + wy[1][1] + wy[2][2]
    doty = [dot * y[n] for n in range(3)]
    rows3, rows5 = {}, {}
    for n, (i, j) in enumerate(PAIRS):
        zero3, zero5 = [], [doty[i] * y[j]]
        for m in range(3):
            if lin3[m, n] is not None:
                rows3[8 * m + n] = lin3[m, n]
                zero3.append(lin3[m, n] * y[m])
            quad = [wy[m][i] * y[j]]
            if m == i:
                quad.append(doty[j])
            if m == j:
                quad.append(doty[i])
            if lin5[m, n] is not None:
                quad.append(lin5[m, n])
                zero5.append(lin5[m, n] * y[m])
            rows5[8 * m + n] = plus(quad)
        if zero3:
            rows3[24 + n] = -plus(zero3)
        rows5[24 + n] = -plus(zero5)
    for m in range(3):
        for n in range(3):
            rows5[32 + 3 * m + n] = -wy[m][n]
        rows5[41 + m] = w3[m]
    return rows3, rows5


def halves(value, terms):
    out = []
    for k in range(terms):
        part = value.astype(jnp.bfloat16)
        out.append(part)
        if k + 1 < terms:
            value = value - part.astype(jnp.float32)
    return out


def near_kernel(planes, before_ref, middle_ref, after_ref, total, raw, feat, wide, left3, left5, own, live_ref, own_live):
    sources = (before_ref, middle_ref, after_ref)
    cells = planes - 2
    columns = [(k, c) for k in range(3) for c in range(3)]
    blocks = -(-(2 * len(columns) + 1) // 8) * 8
    lane = lax.broadcasted_iota(jnp.int32, (ROWS, LANES), 1)
    lift = lax.broadcasted_iota(jnp.int32, (ROWS, LANES), 0)
    raw[...] = jnp.zeros_like(raw)
    feat[...] = jnp.zeros_like(feat)
    total[...] = jnp.zeros_like(total)

    for j in range(planes):
        at = jnp.int32(0)
        for k, c in columns:
            row = ROWS * (c * planes + j)
            shift = (
                jnp.where(lift < 3, -0.5, 0.0)
                + jnp.where(lift == 1, float(c - 1), 0.0)
                + jnp.where(lift == 2, float(k - 1), 0.0)
            )
            first = sources[k][row: row + ROWS, 0:LANES]
            second = sources[k][row: row + ROWS, LANES:]
            count = first[ROWS - 1: ROWS, 0:1].astype(jnp.int32)[0, 0]
            if k == 1 and c == 1 and 0 < j < planes - 1:
                own[j - 1, 0:ROWS, 0:LANES] = first
                own[j - 1, 0:ROWS, LANES:] = second
                own_live[j - 1] = count
            low = jnp.bitwise_and(at, LANES - 1)
            base = lax.shift_right_logical(at, 7) + j * blocks
            first = pltpu.roll(first + shift, low, 1)
            second = pltpu.roll(second + shift, low, 1)
            keep = lane >= low
            place = pl.multiple_of(base * 16, 16)
            raw[pl.ds(place, ROWS), :] = jnp.where(keep, first, raw[pl.ds(place, ROWS), :])
            raw[pl.ds(place + 16, ROWS), :] = jnp.where(keep, second, first)
            raw[pl.ds(place + 32, ROWS), :] = jnp.where(keep, 0.0, second)
            at = at + count
        live_ref[j] = at

    def plane_body(j, carry):
        live = live_ref[j]
        groups = lax.shift_right_logical(live + 8 * LANES - 1, 10)
        steps = lax.shift_right_logical(live + CAP - 1, 8)

        def group_body(g, carry):
            start = pl.multiple_of((j * blocks + g * 8) * 16, 128)
            row = [raw[pl.ds(start + r, 8, stride=16), :] for r in range(9)]
            rows3, rows5 = features(row[0:3], row[3:6], row[6:9])
            for r, value in rows3.items():
                feat[pl.ds(r, 8, stride=NUM3 + NUM5), :] = value
            for r, value in rows5.items():
                feat[pl.ds(NUM3 + r, 8, stride=NUM3 + NUM5), :] = value

            def chunk_body(c, carry):
                for h in range(2):
                    q = (c - g * 4) * 2 + h
                    span = slice(h * LANES, (h + 1) * LANES)
                    at = pl.multiple_of(q * (NUM3 + NUM5), 16)
                    piece = halves(feat[pl.ds(at, NUM3), :], 3)
                    for n in range(3):
                        left3[c, n * NUM3: (n + 1) * NUM3, span] = piece[n]
                    piece = halves(feat[pl.ds(at + NUM3, NUM5), :], 3)
                    for n in range(3):
                        left5[c, n * NUM5: (n + 1) * NUM5, span] = piece[n]
                    turned = jnp.transpose(raw[pl.ds(pl.multiple_of(start + q * 16, 16), 8), :])
                    for n in range(3):
                        wide[c, n, span, :] = jnp.broadcast_to(turned[:, n: n + 1], (LANES, LANES))
                return carry

            lax.fori_loop(g * 4, jnp.minimum(g * 4 + 4, steps), chunk_body, 0)
            return carry

        lax.fori_loop(0, groups, group_body, 0)

        def cell_body(i, carry):
            where_x = (i + 1 - j).astype(jnp.float32) - 0.5
            points = [
                own[i, 0:1, :] + where_x,
                own[i, 1:2, :] - 0.5,
                own[i, 2:3, :] - 0.5,
            ]
            targets = own_live[i]

            def run(parts):
                width = parts * LANES
                seen = [
                    [jnp.broadcast_to(v[:, h * LANES:(h + 1) * LANES], (16, LANES)) for v in points]
                    for h in range(parts)
                ]

                def step(c, acc):
                    acc3, acc5 = acc
                    high3, low3, high5, low5 = [], [], [], []
                    for s in range(CAP // 16):
                        there = [wide[c, n, s * 16: (s + 1) * 16, :] for n in range(3)]
                        got = [[], [], [], []]
                        for h in range(parts):
                            d = [seen[h][n] - there[n] for n in range(3)]
                            inv = lax.rsqrt(d[0] * d[0] + d[1] * d[1] + (d[2] * d[2] + CORE_SQUARE))
                            square = inv * inv
                            cube = square * inv
                            fifth = cube * square
                            a, b = halves(cube, 2)
                            e, f = halves(fifth, 2)
                            for store, value in zip(got, (a, b, e, f)):
                                store.append(value)
                        for store, value in zip((high3, low3, high5, low5), got):
                            store.append(jnp.concatenate(value, axis=1) if parts > 1 else value[0])
                    high3, low3, high5, low5 = [
                        jnp.concatenate(v, axis=0) for v in (high3, low3, high5, low5)
                    ]
                    mm = functools.partial(jnp.dot, preferred_element_type=jnp.float32)
                    a = mm(left3[c], high3)
                    b = mm(left3[c, 0:2 * NUM3, :], low3)
                    acc3 = acc3 + (
                        a[0:NUM3]
                        + (a[NUM3:2 * NUM3] + b[0:NUM3])
                        + (a[2 * NUM3:] + b[NUM3:])
                    )
                    a = mm(left5[c], high5)
                    b = mm(left5[c, 0:2 * NUM5, :], low5)
                    acc5 = acc5 + (
                        a[0:NUM5]
                        + (a[NUM5:2 * NUM5] + b[0:NUM5])
                        + (a[2 * NUM5:] + b[NUM5:])
                    )
                    return acc3, acc5

                acc3, acc5 = lax.fori_loop(
                    0,
                    steps,
                    step,
                    (jnp.zeros((NUM3, width), jnp.float32), jnp.zeros((NUM5, width), jnp.float32)),
                )
                x = [v[:, 0:width] for v in points]
                both = acc3 + acc5[0:NUM3]
                linear = both[24:32] + x[0] * both[0:8] + x[1] * both[8:16] + x[2] * both[16:24]
                second = acc5[32:48]
                v = [
                    x[0] * second[n: n + 1] + x[1] * second[3 + n: 4 + n] + x[2] * second[6 + n: 7 + n]
                    for n in range(3)
                ]
                scale = 0.5 * (
                    second[0:1] + second[4:5] + second[8:9]
                    + x[0] * second[9:10] + x[1] * second[10:11] + x[2] * second[11:12]
                )
                v = [v[n] + scale * x[n] for n in range(3)]
                for n, (a, b) in enumerate(PAIRS):
                    total[i, n: n + 1, 0:width] += linear[n: n + 1] + x[a] * v[b] + x[b] * v[a]

            @pl.when(targets > LANES)
            def _():
                run(2)

            @pl.when(targets <= LANES)
            def _():
                run(1)

            return carry

        lax.fori_loop(jnp.maximum(j - 2, 0), jnp.minimum(j + 1, planes - 2), cell_body, 0)
        return carry

    lax.fori_loop(0, planes, plane_body, 0)


def far_kernel(planes, spans, place_ref, moment_ref, applied_ref, sheet_ref, total, out_ref):
    cells = planes - 2
    span_x, span_y, span_z = spans
    shape = (span_z, LANES)
    moment = [moment_ref[pl.ds(m, span_z, stride=16), :] for m in range(9)]
    column = lax.broadcasted_iota(jnp.int32, shape, 1)
    device = column // cells
    source = (
        (device // span_y * cells + column % cells).astype(jnp.float32),
        (device % span_y).astype(jnp.float32),
        lax.broadcasted_iota(jnp.int32, shape, 0).astype(jnp.float32),
    )
    w = (moment[5] - moment[7], moment[6] - moment[2], moment[1] - moment[3])
    index = {}
    for n, (a, b) in enumerate(PAIRS):
        index[a, b] = index[b, a] = n
    for i in range(cells):
        mine = (place_ref[0] * cells + i, place_ref[1], place_ref[2])
        r = [mine[n].astype(jnp.float32) - source[n] for n in range(3)]
        reach = jnp.maximum(jnp.maximum(jnp.abs(r[0]), jnp.abs(r[1])), jnp.abs(r[2]))
        inv = lax.rsqrt(r[0] * r[0] + r[1] * r[1] + r[2] * r[2] + CORE_SQUARE)
        inv = jnp.where(reach > 1.5, inv, 0.0)
        cube = inv * inv * inv
        fifth = cube * inv * inv
        radial = 2.0 * cube + KAPPA * fifth
        along = w[0] * r[0] + w[1] * r[1] + w[2] * r[2]
        turn = [cross(r, (moment[n], moment[3 + n], moment[6 + n])) for n in range(3)]
        slope = (3.0 * SECOND) * along * fifth
        cut = SECOND * cube
        bulk = SECOND * along * (radial - cube)
        front = -FIRST * radial
        stress = []
        for n, (a, b) in enumerate(PAIRS):
            element = (
                front * (turn[b][a] + turn[a][b])
                + slope * r[a] * r[b]
                - cut * (w[a] * r[b] + w[b] * r[a])
            )
            if a == b:
                element = element + bulk
            stress.append(
                jnp.sum(element, axis=(0, 1), keepdims=True)
                + 0.5 * (applied_ref[a, b] + applied_ref[b, a])
                + total[i, n: n + 1, :]
            )
        row = ROWS * (planes + 1 + i)
        t = [sheet_ref[row + 3 + n: row + 4 + n, :] for n in range(3)]
        b = [sheet_ref[row + 6 + n: row + 7 + n, :] for n in range(3)]
        force = [plus([stress[index[m, n]] * b[n] for n in range(3)]) for m in range(3)]
        for n, value in enumerate(cross(force, t)):
            out_ref[n, i: i + 1, :] = value


def pick_kernel(planes, spans, place_ref, all_ref, sheet_ref, moment_ref):
    span_x, span_y, span_z = spans
    cells = planes - 2
    for dy in range(3):
        y = place_ref[1] + (dy - 1)
        for j in range(planes):
            step = (j + cells - 1) // cells - 1
            c = (j - 1) % cells
            x = place_ref[0] + step
            inside = (x >= 0) & (x < span_x) & (y >= 0) & (y < span_y)
            device = jnp.clip(x, 0, span_x - 1) * span_y + jnp.clip(y, 0, span_y - 1)
            row = ROWS * (dy * planes + j)
            sheet_ref[row: row + ROWS, :] = jnp.where(
                inside, all_ref[device, ROWS * c: ROWS * c + ROWS, :], 0.0
            )
    rows = [
        all_ref[d, ROWS * c + ROWS - 1: ROWS * c + ROWS, LANES:]
        for d in range(span_x * span_y)
        for c in range(cells)
    ]
    rows.append(jnp.zeros((LANES - len(rows), LANES), jnp.float32))
    moment_ref[...] = jnp.transpose(jnp.concatenate(rows, axis=0))[0:16, :]


def local(seg_offset, seg_vector, burgers, cell_counts, applied):
    cells = seg_offset.shape[1]
    planes = cells + 2
    spans = tuple(lax.axis_size(a) for a in ("gx", "gy", "gz"))
    place = jnp.stack([lax.axis_index(a) for a in ("gx", "gy", "gz")]).astype(jnp.int32)
    counts = cell_counts.reshape(cells)
    slots = jnp.arange(CAP, dtype=jnp.int32)
    filled = slots[None, :] < counts[:, None]
    offset = seg_offset.reshape(3, cells, CAP)
    tangent = jnp.where(filled[None], seg_vector.reshape(3, cells, CAP), 0.0)
    charge = jnp.where(filled[None], burgers.reshape(3, cells, CAP), 0.0)
    moment = jnp.sum(charge[:, None] * tangent[None, :], axis=-1).reshape(9, cells).T
    level = jnp.broadcast_to(counts.astype(jnp.float32)[:, None], (cells, LANES))
    level = jnp.concatenate([level, moment, jnp.zeros((cells, LANES - 9), jnp.float32)], axis=1)
    packed = jnp.concatenate([offset, tangent, charge, level[None]]).transpose(1, 0, 2)
    packed = packed.reshape(cells * ROWS, CAP)

    devices = spans[0] * spans[1]
    every = lax.all_to_all(
        jnp.broadcast_to(packed[None], (devices,) + packed.shape), ("gx", "gy"), 0, 0
    )
    vmem = pl.BlockSpec(memory_space=pltpu.VMEM)
    smem = pl.BlockSpec(memory_space=pltpu.SMEM)
    limit = pltpu.CompilerParams(vmem_limit_bytes=40 * 1024 * 1024)
    sheet, moments = pl.pallas_call(
        functools.partial(pick_kernel, planes, spans),
        out_shape=(
            jax.ShapeDtypeStruct((3 * planes * ROWS, CAP), jnp.float32),
            jax.ShapeDtypeStruct((16, LANES), jnp.float32),
        ),
        in_specs=[smem, vmem],
        out_specs=(vmem, vmem),
        compiler_params=limit,
        name="pick",
    )(place, every)
    up = [(i, i + 1) for i in range(spans[2] - 1)]
    down = [(i + 1, i) for i in range(spans[2] - 1)]
    before = lax.ppermute(sheet, "gz", up)
    after = lax.ppermute(sheet, "gz", down)
    moments = lax.all_to_all(
        jnp.broadcast_to(moments[None], (spans[2],) + moments.shape), "gz", 0, 0
    ).reshape(spans[2] * 16, LANES)

    blocks = 24
    total = pl.pallas_call(
        functools.partial(near_kernel, planes),
        out_shape=jax.ShapeDtypeStruct((cells, 8, CAP), jnp.float32),
        in_specs=[vmem, vmem, vmem],
        out_specs=vmem,
        scratch_shapes=[
            pltpu.VMEM((planes * blocks * 16, LANES), jnp.float32),
            pltpu.VMEM((8 * (NUM3 + NUM5), LANES), jnp.float32),
            pltpu.VMEM((blocks // 2, 3, CAP, LANES), jnp.float32),
            pltpu.VMEM((blocks // 2, 3 * NUM3, CAP), jnp.bfloat16),
            pltpu.VMEM((blocks // 2, 3 * NUM5, CAP), jnp.bfloat16),
            pltpu.VMEM((cells, 16, CAP), jnp.float32),
            pltpu.SMEM((planes,), jnp.int32),
            pltpu.SMEM((cells,), jnp.int32),
        ],
        compiler_params=limit,
        cost_estimate=pl.CostEstimate(flops=10**9, bytes_accessed=10**7, transcendentals=0),
        name="near",
    )(before, sheet, after)
    result = pl.pallas_call(
        functools.partial(far_kernel, planes, spans),
        out_shape=jax.ShapeDtypeStruct((3, cells, CAP), jnp.float32),
        in_specs=[smem, vmem, smem, vmem, vmem],
        out_specs=vmem,
        compiler_params=limit,
        name="far",
    )(place, moments, applied, sheet, total)
    return result.reshape(seg_offset.shape)


def solution(mesh):
    placed = P(None, "gx", "gy", "gz", None)
    return jax.shard_map(
        local,
        mesh=mesh,
        in_specs=(placed, placed, placed, P("gx", "gy", "gz"), P()),
        out_specs=placed,
        check_vma=False,
    )
```

```python
import functools
import math

import jax
import jax.numpy as jnp
from jax import lax
from jax.experimental import pallas as pl
from jax.experimental.pallas import tpu as pltpu
from jax.sharding import PartitionSpec as P

CORE_SQUARE = 0.2 * 0.2
FIRST = 1.0 / (8.0 * math.pi)
SECOND = 1.0 / (4.0 * math.pi * 0.7)
KAPPA = 3.0 * CORE_SQUARE
CAP = 256
LANES = 128
ROWS = 10
PAIRS = ((0, 0), (0, 1), (0, 2), (1, 1), (1, 2), (2, 2))
NUM3 = 32
NUM5 = 48
BLOCKS = 24
CHUNKS = 9
TILES = 4


def cross(a, b):
    return (
        a[1] * b[2] - a[2] * b[1],
        a[2] * b[0] - a[0] * b[2],
        a[0] * b[1] - a[1] * b[0],
    )


def plus(terms):
    terms = [t for t in terms if t is not None]
    total = terms[0]
    for t in terms[1:]:
        total = total + t
    return total


def features(y, t, b):
    w = cross(b, t)
    turn = [[None, b[2], -b[1]], [-b[2], None, b[0]], [b[1], -b[0], None]]
    c2w = [SECOND * v for v in w]
    lin3, lin5 = {}, {}
    for n, (i, j) in enumerate(PAIRS):
        for m in range(3):
            parts = []
            if turn[i][m] is not None:
                parts.append(turn[i][m] * t[j])
            if turn[j][m] is not None:
                parts.append(turn[j][m] * t[i])
            base = plus(parts) * (-FIRST) if parts else None
            a3 = [2.0 * base] if base is not None else []
            a5 = [base] if base is not None else []
            if i == j:
                a3.append(c2w[m])
                a5.append(c2w[m])
            if m == j:
                a3.append(-c2w[i])
            if m == i:
                a3.append(-c2w[j])
            lin3[m, n] = plus(a3) if a3 else None
            lin5[m, n] = KAPPA * plus(a5) if a5 else None
    w3 = [3.0 * v for v in c2w]
    wy = [[w3[m] * y[n] for n in range(3)] for m in range(3)]
    dot = wy[0][0] + wy[1][1] + wy[2][2]
    doty = [dot * y[n] for n in range(3)]
    rows3, rows5 = {}, {}
    for n, (i, j) in enumerate(PAIRS):
        zero3, zero5 = [], [doty[i] * y[j]]
        for m in range(3):
            if lin3[m, n] is not None:
                rows3[8 * m + n] = lin3[m, n]
                zero3.append(lin3[m, n] * y[m])
            quad = [wy[m][i] * y[j]]
            if m == i:
                quad.append(doty[j])
            if m == j:
                quad.append(doty[i])
            if lin5[m, n] is not None:
                quad.append(lin5[m, n])
                zero5.append(lin5[m, n] * y[m])
            rows5[8 * m + n] = plus(quad)
        if zero3:
            rows3[24 + n] = -plus(zero3)
        rows5[24 + n] = -plus(zero5)
    for m in range(3):
        for n in range(3):
            rows5[32 + 3 * m + n] = -wy[m][n]
        rows5[41 + m] = w3[m]
    return rows3, rows5


def halves(value, terms):
    out = []
    for k in range(terms):
        part = value.astype(jnp.bfloat16)
        out.append(part)
        if k + 1 < terms:
            value = value - part.astype(jnp.float32)
    return out


def near_kernel(
    planes, before_ref, middle_ref, after_ref, out_ref,
    raw, feat, cols, left3, left5, left_d, right_d, line,
    buf_a, buf_b, acc, aim, total, steps_ref, starts_ref, span_ref,
):
    sources = (before_ref, middle_ref, after_ref)
    cells = planes - 2
    columns = [(k, c) for k in range(3) for c in range(3)]
    lane = lax.broadcasted_iota(jnp.int32, (16, LANES), 1)
    lift = lax.broadcasted_iota(jnp.int32, (16, LANES), 0)
    mm = functools.partial(jnp.dot, preferred_element_type=jnp.float32)
    for ref in (raw, feat, cols, acc, aim, total, line):
        ref[...] = jnp.zeros_like(ref)

    def append(ref, first, second, at, offset):
        rows = first.shape[0]
        low = jnp.bitwise_and(at, LANES - 1)
        base = lax.shift_right_logical(at, 7) + offset
        first = pltpu.roll(first, low, 1)
        second = pltpu.roll(second, low, 1)
        keep = lane[0:rows] >= low
        place = pl.multiple_of(base * 16, 16)
        ref[pl.ds(place, rows), :] = jnp.where(keep, first, ref[pl.ds(place, rows), :])
        ref[pl.ds(place + 16, rows), :] = jnp.where(keep, second, first)
        ref[pl.ds(place + 32, rows), :] = jnp.where(keep, 0.0, second)

    goal = jnp.int32(0)
    for j in range(planes):
        at = jnp.int32(0)
        for k, c in columns:
            row = ROWS * (c * planes + j)
            first = sources[k][row: row + ROWS, 0:LANES]
            second = sources[k][row: row + ROWS, LANES:]
            count = first[ROWS - 1: ROWS, 0:1].astype(jnp.int32)[0, 0]
            if k == 1 and c == 1 and 0 < j < planes - 1:
                shift = jnp.where(lift[0:8] == 0, j - 0.5, -0.5)
                mark = lift[0:8] < 3
                starts_ref[j - 1] = goal
                append(
                    aim,
                    jnp.where(mark, first[0:8] + shift, float(j)),
                    jnp.where(mark, second[0:8] + shift, float(j)),
                    goal,
                    0,
                )
                goal = goal + count
            shift = (
                jnp.where(lift < 3, -0.5, 0.0)
                + jnp.where(lift == 1, float(c - 1), 0.0)
                + jnp.where(lift == 2, float(k - 1), 0.0)
            )[0:ROWS]
            append(raw, first + shift, second + shift, at, j * BLOCKS)
            at = at + count
        steps_ref[j] = jnp.maximum(lax.shift_right_logical(at + CAP - 1, 8), 1)
    starts_ref[cells] = goal
    for j in range(planes):
        span_ref[j, 0] = lax.shift_right_logical(starts_ref[max(j - 2, 0)], 8)
        span_ref[j, 1] = lax.shift_right_logical(starts_ref[min(j, cells - 1) + 1] + CAP - 1, 8)

    def target(tile):
        at = pl.multiple_of(tile * 32, 32)
        return jnp.concatenate([aim[pl.ds(at, 8), :], aim[pl.ds(at + 16, 8), :]], axis=1)

    def plane_body(j, carry):
        plane = j.astype(jnp.float32)
        steps = steps_ref[j]

        def tile_body(tile, carry):
            spot = target(tile)
            x = [spot[0:1] - plane, spot[1:2], spot[2:3]]
            size = x[0] * x[0] + x[1] * x[1] + x[2] * x[2]
            size = jnp.where(jnp.abs(spot[3:4] - plane) < 1.5, size, 1e30)
            for n in range(3):
                part = [v.astype(jnp.float32) for v in halves(-2.0 * x[n], 3)]
                for r, p in enumerate((0, 1, 0, 1, 2, 0)):
                    line[6 * n + r: 6 * n + r + 1, :] = part[p]
            line[18:21, :] = jnp.ones((3, CAP), jnp.float32)
            for r, p in enumerate(halves(size, 3)):
                line[21 + r: 22 + r, :] = p.astype(jnp.float32)
            right_d[j * TILES + tile] = line[...].astype(jnp.bfloat16)
            return carry

        lax.fori_loop(span_ref[j, 0], span_ref[j, 1], tile_body, 0)

        def group_body(g, carry):
            start = pl.multiple_of((j * BLOCKS + g * 8) * 16, 128)
            row = [raw[pl.ds(start + r, 8, stride=16), :] for r in range(9)]
            y = row[0:3]
            rows3, rows5 = features(y, row[3:6], row[6:9])
            for r, value in rows3.items():
                feat[pl.ds(r, 8, stride=NUM3 + NUM5), :] = value
            for r, value in rows5.items():
                feat[pl.ds(NUM3 + r, 8, stride=NUM3 + NUM5), :] = value
            for n in range(3):
                part = [v.astype(jnp.float32) for v in halves(y[n], 3)]
                for r, p in enumerate((0, 0, 1, 1, 0, 2)):
                    cols[pl.ds(6 * n + r, 8, stride=32), :] = part[p]
            size = y[0] * y[0] + y[1] * y[1] + (y[2] * y[2] + CORE_SQUARE)
            for r, p in enumerate(halves(size, 3)):
                cols[pl.ds(18 + r, 8, stride=32), :] = p.astype(jnp.float32)
            for r in range(3):
                cols[pl.ds(21 + r, 8, stride=32), :] = jnp.ones((8, LANES), jnp.float32)

            def chunk_body(c, carry):
                index = j * CHUNKS + c
                for h in range(2):
                    q = (c - g * 4) * 2 + h
                    span = slice(h * LANES, (h + 1) * LANES)
                    at = pl.multiple_of(q * (NUM3 + NUM5), 16)
                    piece = halves(feat[pl.ds(at, NUM3), :], 3)
                    for n in range(3):
                        left3[index, n * NUM3: (n + 1) * NUM3, span] = piece[n]
                    piece = halves(feat[pl.ds(at + NUM3, NUM5), :], 3)
                    for n in range(3):
                        left5[index, n * NUM5: (n + 1) * NUM5, span] = piece[n]
                    turned = jnp.transpose(cols[pl.ds(pl.multiple_of(q * 32, 32), 32), :])
                    left_d[index, span, :] = turned.astype(jnp.bfloat16)
                return carry

            lax.fori_loop(g * 4, jnp.minimum(g * 4 + 4, steps), chunk_body, 0)
            return carry

        lax.fori_loop(0, lax.shift_right_logical(steps + 3, 2), group_body, 0)
        return carry

    lax.fori_loop(0, planes, plane_body, 0)

    def advance(item):
        j, tile, c = item
        wrap = c + 1 >= steps_ref[j]
        turn = wrap & (tile + 1 >= span_ref[j, 1])
        end = turn & (j + 1 >= planes)
        later = jnp.minimum(j + 1, planes - 1)
        new_j = jnp.where(turn, later, j)
        new_tile = jnp.where(turn, span_ref[later, 0], jnp.where(wrap, tile + 1, tile))
        new_c = jnp.where(wrap, 0, c + 1)
        return (new_j, jnp.where(end, tile, new_tile), jnp.where(end, c, new_c))

    def weigh(item, buf):
        j, tile, c = item
        apart = mm(left_d[j * CHUNKS + c], right_d[j * TILES + tile])
        for s in range(CAP // 16):
            span = slice(s * 16, (s + 1) * 16)
            inv = lax.rsqrt(apart[span, :])
            square = inv * inv
            cube = square * inv
            fifth = cube * square
            buf[0, span, :], buf[1, span, :] = halves(cube, 2)
            buf[2, span, :], buf[3, span, :] = halves(fifth, 2)

    def gather(item, buf, live):
        j, tile, c = item
        index = j * CHUNKS + c
        slot = jnp.where(live, j * TILES + tile, planes * TILES)
        a = mm(left3[index], buf[0])
        b = mm(left3[index, 0:2 * NUM3, :], buf[1])
        acc[slot, 0:NUM3, :] += (
            a[0:NUM3] + (a[NUM3:2 * NUM3] + b[0:NUM3]) + (a[2 * NUM3:] + b[NUM3:])
        )
        a = mm(left5[index], buf[2])
        b = mm(left5[index, 0:2 * NUM5, :], buf[3])
        acc[slot, NUM3:, :] += (
            a[0:NUM5] + (a[NUM5:2 * NUM5] + b[0:NUM5]) + (a[2 * NUM5:] + b[NUM5:])
        )

    count = jnp.int32(0)
    for j in range(planes):
        count = count + steps_ref[j] * (span_ref[j, 1] - span_ref[j, 0])

    def work(m, item):
        after = advance(item)
        weigh(after, buf_b)
        gather(item, buf_a, True)
        later = advance(after)
        weigh(later, buf_a)
        gather(after, buf_b, 2 * m + 1 < count)
        return later

    first = (jnp.int32(0), span_ref[0, 0], jnp.int32(0))
    weigh(first, buf_a)
    lax.fori_loop(0, lax.shift_right_logical(count + 1, 1), work, first)

    def finish_plane(j, carry):
        plane = j.astype(jnp.float32)

        def finish(tile, carry):
            spot = target(tile)
            x = [spot[0:1] - plane, spot[1:2], spot[2:3]]
            slot = j * TILES + tile
            both = acc[slot, 0:NUM3, :] + acc[slot, NUM3:2 * NUM3, :]
            linear = both[24:32] + x[0] * both[0:8] + x[1] * both[8:16] + x[2] * both[16:24]
            second = acc[slot, 2 * NUM3:, :]
            v = [
                x[0] * second[n: n + 1] + x[1] * second[3 + n: 4 + n] + x[2] * second[6 + n: 7 + n]
                for n in range(3)
            ]
            scale = 0.5 * (
                second[0:1] + second[4:5] + second[8:9]
                + x[0] * second[9:10] + x[1] * second[10:11] + x[2] * second[11:12]
            )
            v = [v[n] + scale * x[n] for n in range(3)]
            bend = jnp.concatenate(
                [x[a] * v[b] + x[b] * v[a] for a, b in PAIRS] + [jnp.zeros((2, CAP), jnp.float32)],
                axis=0,
            )
            value = linear + bend
            at = pl.multiple_of(tile * 16, 16)
            total[pl.ds(at, 8), :] += value[:, 0:LANES]
            total[pl.ds(at + 8, 8), :] += value[:, LANES:]
            return carry

        lax.fori_loop(span_ref[j, 0], span_ref[j, 1], finish, 0)
        return carry

    lax.fori_loop(0, planes, finish_plane, 0)

    for i in range(cells):
        at = starts_ref[i]
        low = jnp.bitwise_and(at, LANES - 1)
        back = jnp.bitwise_and(LANES - low, LANES - 1)
        place = pl.multiple_of(lax.shift_right_logical(at, 7) * 8, 8)
        part = [pltpu.roll(total[pl.ds(place + 8 * n, 8), :], back, 1) for n in range(3)]
        keep = lane[0:8] < LANES - low
        out_ref[i, :, 0:LANES] = jnp.where(keep, part[0], part[1])
        out_ref[i, :, LANES:] = jnp.where(keep, part[1], part[2])


def near_call(before, sheet, after):
    planes = sheet.shape[0] // (3 * ROWS)
    cells = planes - 2
    vmem = pl.BlockSpec(memory_space=pltpu.VMEM)
    return pl.pallas_call(
        functools.partial(near_kernel, planes),
        out_shape=jax.ShapeDtypeStruct((cells, 8, CAP), jnp.float32),
        in_specs=[vmem, vmem, vmem],
        out_specs=vmem,
        scratch_shapes=[
            pltpu.VMEM((planes * BLOCKS * 16, LANES), jnp.float32),
            pltpu.VMEM((8 * (NUM3 + NUM5), LANES), jnp.float32),
            pltpu.VMEM((8 * 32, LANES), jnp.float32),
            pltpu.VMEM((planes * CHUNKS, 3 * NUM3, CAP), jnp.bfloat16),
            pltpu.VMEM((planes * CHUNKS, 3 * NUM5, CAP), jnp.bfloat16),
            pltpu.VMEM((planes * CHUNKS, CAP, 32), jnp.bfloat16),
            pltpu.VMEM((planes * TILES, 32, CAP), jnp.bfloat16),
            pltpu.VMEM((32, CAP), jnp.float32),
            pltpu.VMEM((4, CAP, CAP), jnp.bfloat16),
            pltpu.VMEM((4, CAP, CAP), jnp.bfloat16),
            pltpu.VMEM((planes * TILES + 1, NUM3 + NUM5, CAP), jnp.float32),
            pltpu.VMEM((10 * 16, LANES), jnp.float32),
            pltpu.VMEM((10 * 8, LANES), jnp.float32),
            pltpu.SMEM((planes,), jnp.int32),
            pltpu.SMEM((cells + 1,), jnp.int32),
            pltpu.SMEM((planes, 2), jnp.int32),
        ],
        compiler_params=pltpu.CompilerParams(vmem_limit_bytes=40 * 1024 * 1024),
        cost_estimate=pl.CostEstimate(flops=10**9, bytes_accessed=10**7, transcendentals=0),
        name="near",
    )(before, sheet, after)


def far_kernel(planes, spans, place_ref, moment_ref, applied_ref, sheet_ref, total, out_ref):
    cells = planes - 2
    span_x, span_y, span_z = spans
    shape = (span_z, LANES)
    half = LANES // 2
    column = lax.broadcasted_iota(jnp.int32, shape, 1)
    moment = []
    for m in range(9):
        value = moment_ref[:, 0, m // 2 * LANES: (m // 2 + 1) * LANES]
        if m % 2:
            value = pltpu.roll(value, half, 1)
        moment.append(jnp.where(column < half, value, 0.0))
    device = column // cells
    source = (
        (device // span_y * cells + column % cells).astype(jnp.float32),
        (device % span_y).astype(jnp.float32),
        lax.broadcasted_iota(jnp.int32, shape, 0).astype(jnp.float32),
    )
    w = (moment[5] - moment[7], moment[6] - moment[2], moment[1] - moment[3])
    index = {}
    for n, (a, b) in enumerate(PAIRS):
        index[a, b] = index[b, a] = n
    for i in range(cells):
        mine = (place_ref[0] * cells + i, place_ref[1], place_ref[2])
        r = [mine[n].astype(jnp.float32) - source[n] for n in range(3)]
        reach = jnp.maximum(jnp.maximum(jnp.abs(r[0]), jnp.abs(r[1])), jnp.abs(r[2]))
        inv = lax.rsqrt(r[0] * r[0] + r[1] * r[1] + r[2] * r[2] + CORE_SQUARE)
        inv = jnp.where(reach > 1.5, inv, 0.0)
        cube = inv * inv * inv
        fifth = cube * inv * inv
        radial = 2.0 * cube + KAPPA * fifth
        along = w[0] * r[0] + w[1] * r[1] + w[2] * r[2]
        turn = [cross(r, (moment[n], moment[3 + n], moment[6 + n])) for n in range(3)]
        slope = (3.0 * SECOND) * along * fifth
        cut = SECOND * cube
        bulk = SECOND * along * (radial - cube)
        front = -FIRST * radial
        stress = []
        for n, (a, b) in enumerate(PAIRS):
            element = (
                front * (turn[b][a] + turn[a][b])
                + slope * r[a] * r[b]
                - cut * (w[a] * r[b] + w[b] * r[a])
            )
            if a == b:
                element = element + bulk
            stress.append(
                jnp.sum(element, axis=(0, 1), keepdims=True)
                + 0.5 * (applied_ref[a, b] + applied_ref[b, a])
                + total[i, n: n + 1, :]
            )
        row = ROWS * (planes + 1 + i)
        t = [sheet_ref[row + 3 + n: row + 4 + n, :] for n in range(3)]
        b = [sheet_ref[row + 6 + n: row + 7 + n, :] for n in range(3)]
        force = [plus([stress[index[m, n]] * b[n] for n in range(3)]) for m in range(3)]
        for n, value in enumerate(cross(force, t)):
            out_ref[n, i, 0, :, :] = value


def pack_kernel(counts_ref, offset_ref, vector_ref, burgers_ref, all_ref, hold, sems):
    cells = offset_ref.shape[1]
    copies = [
        pltpu.make_async_copy(ref, hold.at[n], sems.at[n])
        for n, ref in enumerate((offset_ref, vector_ref, burgers_ref))
    ]
    for copy in copies:
        copy.start()
    slot = lax.broadcasted_iota(jnp.int32, (cells, CAP), 1)
    cell = lax.broadcasted_iota(jnp.int32, (cells, CAP), 0)
    live = jnp.zeros((cells, CAP), jnp.int32)
    for i in range(cells):
        live = jnp.where(cell == i, counts_ref[i], live)
    filled = slot < live
    for copy in copies:
        copy.wait()
    flat = [hold[n].reshape(3, cells, CAP) for n in range(3)]
    offset = [flat[0][n] for n in range(3)]
    tangent = [jnp.where(filled, flat[1][n], 0.0) for n in range(3)]
    charge = [jnp.where(filled, flat[2][n], 0.0) for n in range(3)]
    level = live.astype(jnp.float32)
    for m in range(3):
        for k in range(3):
            value = jnp.sum(charge[m] * tangent[k], axis=1, keepdims=True)
            level = jnp.where(slot == LANES + 3 * m + k, value, level)
    rows = offset + tangent + charge + [level]
    packed = jnp.concatenate([v[i: i + 1] for i in range(cells) for v in rows], axis=0)
    for d in range(all_ref.shape[0]):
        all_ref[d] = packed


def pick_kernel(planes, spans, place_ref, all_ref, sheet_ref, moment_ref):
    span_x, span_y, span_z = spans
    cells = planes - 2
    for dy in range(3):
        y = place_ref[1] + (dy - 1)
        for j in range(planes):
            step = (j + cells - 1) // cells - 1
            c = (j - 1) % cells
            x = place_ref[0] + step
            inside = (x >= 0) & (x < span_x) & (y >= 0) & (y < span_y)
            device = jnp.clip(x, 0, span_x - 1) * span_y + jnp.clip(y, 0, span_y - 1)
            row = ROWS * (dy * planes + j)
            sheet_ref[row: row + ROWS, :] = jnp.where(
                inside, all_ref[device, ROWS * c: ROWS * c + ROWS, :], 0.0
            )
    rows = [
        all_ref[d, ROWS * c + ROWS - 1: ROWS * c + ROWS, LANES:]
        for d in range(span_x * span_y)
        for c in range(cells)
    ]
    rows.append(jnp.zeros((LANES - len(rows), LANES), jnp.float32))
    flip = jnp.transpose(jnp.concatenate(rows, axis=0))
    half = LANES // 2
    line = [
        flip[2 * r: 2 * r + 1] + pltpu.roll(flip[2 * r + 1: 2 * r + 2], half, 1) for r in range(5)
    ]
    line = jnp.concatenate(line, axis=1)
    moment_ref[...] = jnp.broadcast_to(line[None], moment_ref.shape)


def beside(first, last, axis):
    devices = lax.axis_size(axis)
    up = [(i, i + 1) for i in range(devices - 1)]
    down = [(i + 1, i) for i in range(devices - 1)]
    return lax.ppermute(last, axis, up), lax.ppermute(first, axis, down)


def local(seg_offset, seg_vector, burgers, cell_counts, applied):
    cells = seg_offset.shape[1]
    planes = cells + 2
    spans = tuple(lax.axis_size(a) for a in ("gx", "gy", "gz"))
    place = jnp.stack([lax.axis_index(a) for a in ("gx", "gy", "gz")]).astype(jnp.int32)
    devices = spans[0] * spans[1]
    vmem = pl.BlockSpec(memory_space=pltpu.VMEM)
    smem = pl.BlockSpec(memory_space=pltpu.SMEM)
    anywhere = pl.BlockSpec(memory_space=pl.ANY)
    limit = pltpu.CompilerParams(vmem_limit_bytes=40 * 1024 * 1024)
    packed = pl.pallas_call(
        pack_kernel,
        out_shape=jax.ShapeDtypeStruct((devices, cells * ROWS, CAP), jnp.float32),
        in_specs=[smem] + [anywhere] * 3,
        out_specs=vmem,
        scratch_shapes=[
            pltpu.VMEM((3,) + seg_offset.shape, jnp.float32),
            pltpu.SemaphoreType.DMA((3,)),
        ],
        compiler_params=pltpu.CompilerParams(vmem_limit_bytes=60 * 1024 * 1024),
        name="pack",
    )(cell_counts.reshape(cells), seg_offset, seg_vector, burgers)
    every = lax.all_to_all(packed, ("gx", "gy"), 0, 0)
    sheet, moments = pl.pallas_call(
        functools.partial(pick_kernel, planes, spans),
        out_shape=(
            jax.ShapeDtypeStruct((3 * planes * ROWS, CAP), jnp.float32),
            jax.ShapeDtypeStruct((spans[2], 1, 5 * LANES), jnp.float32),
        ),
        in_specs=[smem, vmem],
        out_specs=(vmem, vmem),
        compiler_params=limit,
        name="pick",
    )(place, every)
    before, after = beside(sheet, sheet, "gz")
    moments = lax.all_to_all(moments, "gz", 0, 0)
    total = near_call(before, sheet, after)
    return pl.pallas_call(
        functools.partial(far_kernel, planes, spans),
        out_shape=jax.ShapeDtypeStruct(seg_offset.shape, jnp.float32),
        in_specs=[smem, vmem, smem, vmem, vmem],
        out_specs=vmem,
        compiler_params=limit,
        name="far",
    )(place, moments, applied, sheet, total)


def solution(mesh):
    placed = P(None, "gx", "gy", "gz", None)
    return jax.shard_map(
        local,
        mesh=mesh,
        in_specs=(placed, placed, placed, P("gx", "gy", "gz"), P()),
        out_specs=placed,
        check_vma=False,
    )
```

```python
import functools
import math

import jax
import jax.numpy as jnp
from jax import lax
from jax.experimental import pallas as pl
from jax.experimental.pallas import tpu as pltpu
from jax.sharding import PartitionSpec as P

CORE_SQUARE = 0.2 * 0.2
FIRST = 1.0 / (8.0 * math.pi)
SECOND = 1.0 / (4.0 * math.pi * 0.7)
KAPPA = 3.0 * CORE_SQUARE
CAP = 256
LANES = 128
ROWS = 10
PAIRS = ((0, 0), (0, 1), (0, 2), (1, 1), (1, 2), (2, 2))
NUM3 = 24
NUM5 = 40
NUM = NUM3 + NUM5
BLOCKS = 24
CHUNKS = 10
TILES = 3


def cross(a, b):
    return (
        a[1] * b[2] - a[2] * b[1],
        a[2] * b[0] - a[0] * b[2],
        a[0] * b[1] - a[1] * b[0],
    )


def plus(terms):
    terms = [t for t in terms if t is not None]
    total = terms[0]
    for t in terms[1:]:
        total = total + t
    return total


def features(y, t, b):
    w = cross(b, t)
    turn = [[None, b[2], -b[1]], [-b[2], None, b[0]], [b[1], -b[0], None]]
    c2w = [SECOND * v for v in w]
    lin3, lin5 = {}, {}
    for n, (i, j) in enumerate(PAIRS):
        for m in range(3):
            parts = []
            if turn[i][m] is not None:
                parts.append(turn[i][m] * t[j])
            if turn[j][m] is not None:
                parts.append(turn[j][m] * t[i])
            base = plus(parts) * (-FIRST) if parts else None
            a3 = [2.0 * base] if base is not None else []
            a5 = [base] if base is not None else []
            if i == j:
                a3.append(c2w[m])
                a5.append(c2w[m])
            if m == j:
                a3.append(-c2w[i])
            if m == i:
                a3.append(-c2w[j])
            lin3[m, n] = plus(a3) if a3 else None
            lin5[m, n] = KAPPA * plus(a5) if a5 else None
    w3 = [3.0 * v for v in c2w]
    wy = [[w3[m] * y[n] for n in range(3)] for m in range(3)]
    dot = wy[0][0] + wy[1][1] + wy[2][2]
    doty = [dot * y[n] for n in range(3)]
    rows3, rows5 = {}, {}
    for n, (i, j) in enumerate(PAIRS):
        zero3, zero5 = [], [doty[i] * y[j]]
        for m in range(3):
            if lin3[m, n] is not None:
                rows3[6 * m + n] = lin3[m, n]
                zero3.append(lin3[m, n] * y[m])
            quad = [wy[m][i] * y[j]]
            if m == i:
                quad.append(doty[j])
            if m == j:
                quad.append(doty[i])
            if lin5[m, n] is not None:
                quad.append(lin5[m, n])
                zero5.append(lin5[m, n] * y[m])
            rows5[6 * m + n] = plus(quad)
        if zero3:
            rows3[18 + n] = -plus(zero3)
        rows5[18 + n] = -plus(zero5)
    for m in range(3):
        for n in range(3):
            rows5[24 + 3 * m + n] = -wy[m][n]
        rows5[33 + m] = w3[m]
    return rows3, rows5


def halves(value, terms):
    out = []
    for k in range(terms):
        part = value.astype(jnp.bfloat16)
        out.append(part)
        if k + 1 < terms:
            value = value - part.astype(jnp.float32)
    return out


def near_kernel(
    planes, before_ref, middle_ref, after_ref, out_ref,
    raw, feat, cols, left3, left5, left_d, right_d, spots, line, buf_a, buf_b, acc, aim, total, steps_ref, starts_ref, tiles_ref,
):
    sources = (before_ref, middle_ref, after_ref)
    cells = planes - 2
    columns = [(k, c) for k in range(3) for c in range(3)]
    lane = lax.broadcasted_iota(jnp.int32, (16, LANES), 1)
    lift = lax.broadcasted_iota(jnp.int32, (16, LANES), 0)
    mm = functools.partial(jnp.dot, preferred_element_type=jnp.float32)
    for ref in (raw, aim, total, line):
        ref[...] = jnp.zeros_like(ref)

    def append(ref, first, second, at, offset):
        rows = first.shape[0]
        low = jnp.bitwise_and(at, LANES - 1)
        base = lax.shift_right_logical(at, 7) + offset
        first = pltpu.roll(first, low, 1)
        second = pltpu.roll(second, low, 1)
        keep = lane[0:rows] >= low
        place = pl.multiple_of(base * 16, 16)
        ref[pl.ds(place, rows), :] = jnp.where(keep, first, ref[pl.ds(place, rows), :])
        ref[pl.ds(place + 16, rows), :] = jnp.where(keep, second, first)
        ref[pl.ds(place + 32, rows), :] = jnp.where(keep, 0.0, second)

    goal = jnp.int32(0)
    for j in range(planes):
        at = jnp.int32(0)
        for k, c in columns:
            row = ROWS * (c * planes + j)
            first = sources[k][row: row + ROWS, 0:LANES]
            second = sources[k][row: row + ROWS, LANES:]
            count = first[ROWS - 1: ROWS, 0:1].astype(jnp.int32)[0, 0]
            if k == 1 and c == 1 and 0 < j < planes - 1:
                shift = jnp.where(lift[0:8] == 0, j - 0.5, -0.5)
                mark = lift[0:8] < 3
                starts_ref[j - 1] = goal
                append(
                    aim,
                    jnp.where(mark, first[0:8] + shift, float(j)),
                    jnp.where(mark, second[0:8] + shift, float(j)),
                    goal,
                    0,
                )
                goal = goal + count
            shift = (
                jnp.where(lift < 3, -0.5, 0.0)
                + jnp.where(lift == 1, float(c - 1), 0.0)
                + jnp.where(lift == 2, float(k - 1), 0.0)
            )[0:ROWS]
            append(raw, first + shift, second + shift, at, j * BLOCKS)
            at = at + count
        steps_ref[j] = jnp.maximum(lax.shift_right_logical(at + CAP - 1, 8), 1)
    starts_ref[cells] = goal
    for j in range(planes):
        reach = starts_ref[min(j, cells - 1) + 1] - starts_ref[max(j - 2, 0)]
        tiles_ref[j] = lax.shift_right_logical(reach + CAP - 1, 8)

    for j in range(planes):
        for tile in range(min(j, cells - 1) + 1 - max(j - 2, 0)):
            at = starts_ref[max(j - 2, 0)] + CAP * tile
            at = jnp.minimum(at, starts_ref[cells])
            low = jnp.bitwise_and(at, LANES - 1)
            back = jnp.bitwise_and(LANES - low, LANES - 1)
            place = pl.multiple_of(lax.shift_right_logical(at, 7) * 16, 16)
            part = [pltpu.roll(aim[pl.ds(place + 16 * n, 8), :], back, 1) for n in range(3)]
            keep = lane[0:8] < LANES - low
            spot = jnp.concatenate(
                [jnp.where(keep, part[0], part[1]), jnp.where(keep, part[1], part[2])], axis=1
            )
            x = [spot[0:1] - float(j), spot[1:2], spot[2:3]]
            size = x[0] * x[0] + x[1] * x[1] + x[2] * x[2]
            size = jnp.where(jnp.abs(spot[3:4] - float(j)) < 1.5, size, 1e30)
            slot = j * TILES + tile
            for n in range(3):
                spots[slot, n: n + 1, :] = x[n]
                part = [v.astype(jnp.float32) for v in halves(-2.0 * x[n], 3)]
                for r, p in enumerate((0, 1, 0, 1, 2, 0)):
                    line[slot, 6 * n + r: 6 * n + r + 1, :] = part[p]
            line[slot, 18:21, :] = jnp.ones((3, CAP), jnp.float32)
            for r, p in enumerate(halves(size, 3)):
                line[slot, 21 + r: 22 + r, :] = p.astype(jnp.float32)
            right_d[slot] = line[slot].astype(jnp.bfloat16)

    def describe(j, g):
        start = (j * BLOCKS + g * 8) * 16
        row = jnp.swapaxes(jnp.stack([raw[start + 16 * q: start + 16 * q + 8, :] for q in range(8)]), 0, 1)
        row = [row[r] for r in range(8)] + [raw[pl.ds(start + 8, 8, stride=16), :]]
        rows3, rows5 = features(row[0:3], row[3:6], row[6:9])
        base = (j * BLOCKS + g * 8) * NUM
        def spread(ref, first, step, rows):
            for k in range(0, len(rows), 8):
                part = jnp.swapaxes(jnp.stack(rows[k: k + 8]), 0, 1)
                for q in range(8):
                    ref[first + q * step + k: first + q * step + k + 8, :] = part[q]

        none = jnp.zeros((8, LANES), jnp.float32)
        spread(feat, base, NUM, [rows3.get(r, none) for r in range(NUM3)] + [rows5.get(r, none) for r in range(NUM5)])
        y = row[0:3]
        size = y[0] * y[0] + y[1] * y[1] + (y[2] * y[2] + CORE_SQUARE)
        line_rows = []
        for n in range(3):
            part = [v.astype(jnp.float32) for v in halves(y[n], 3)]
            line_rows += [part[p] for p in (0, 0, 1, 1, 0, 2)]
        line_rows += [p.astype(jnp.float32) for p in halves(size, 3)]
        line_rows += [none + 1.0] * 3 + [none] * 8
        spread(cols, (j * BLOCKS + g * 8) * 32, 32, line_rows)

    for j in range(planes):
        describe(j, 0)
    for g in range(1, BLOCKS // 8):
        for j in range(planes):
            pl.when(steps_ref[j] > 4 * g)(functools.partial(describe, j, g))

    def rest(value):
        return value - value.astype(jnp.bfloat16).astype(jnp.float32)

    def split_body(n, state):
        j, c = state
        for part in range(2):
            index = j * CHUNKS + c + part
            for h in range(2):
                block = j * BLOCKS + 2 * (c + part) + h
                span = slice(h * LANES, (h + 1) * LANES)
                at = pl.multiple_of(block * NUM, 8)
                value = feat[pl.ds(at, NUM3), :]
                left3[index, :, span] = jnp.concatenate([value, rest(value)], axis=0).astype(
                    jnp.bfloat16
                )
                value = feat[pl.ds(at + NUM3, NUM5), :]
                second = rest(value)
                third = rest(second)
                left5[index, :, span] = jnp.concatenate(
                    [value, second, third, jnp.zeros((8, LANES), jnp.float32)], axis=0
                ).astype(jnp.bfloat16)
                turned = jnp.transpose(cols[pl.ds(pl.multiple_of(block * 32, 32), 32), :])
                left_d[index, span, :] = turned.astype(jnp.bfloat16)
        wrap = c + 2 >= steps_ref[j]
        return (
            jnp.where(wrap, jnp.minimum(j + 1, planes - 1), j),
            jnp.where(wrap, 0, c + 2),
        )

    pieces = jnp.int32(0)
    for j in range(planes):
        pieces = pieces + lax.shift_right_logical(steps_ref[j] + 1, 1)
    lax.fori_loop(0, pieces, split_body, (jnp.int32(0), jnp.int32(0)))

    def advance(item):
        j, tile, c = item
        wrap = c + 1 >= steps_ref[j]
        turn = wrap & (tile + 1 >= tiles_ref[j])
        end = turn & (j + 1 >= planes)
        new_j = jnp.where(turn, jnp.minimum(j + 1, planes - 1), j)
        new_tile = jnp.where(turn, 0, jnp.where(wrap, tile + 1, tile))
        new_c = jnp.where(wrap, 0, c + 1)
        return (new_j, jnp.where(end, tile, new_tile), jnp.where(end, c, new_c))

    def weigh(item, buf):
        j, tile, c = item
        apart = mm(left_d[j * CHUNKS + c], right_d[j * TILES + tile])
        for s in range(CAP // 16):
            span = slice(s * 16, (s + 1) * 16)
            inv = lax.rsqrt(apart[span, :])
            square = inv * inv
            cube = square * inv
            fifth = cube * square
            buf[0, span, :], buf[1, span, :] = halves(cube, 2)
            buf[2, span, :], buf[3, span, :] = halves(fifth, 2)

    def gather(item, buf, live):
        j, tile, c = item
        index = j * CHUNKS + c
        slot = jnp.where(live, j * TILES + tile, planes * TILES)
        a = mm(left3[index], buf[0])
        b = mm(left3[index, 0:32, :], buf[1])
        d = mm(left5[index], buf[2])
        e = mm(left5[index, 0:2 * NUM5, :], buf[3])
        old = jnp.where(c == 0, 0.0, acc[slot])
        acc[slot, 0:NUM3, :] = old[0:NUM3] + (a[0:NUM3] + (a[NUM3:] + b[0:NUM3]))
        acc[slot, NUM3:, :] = old[NUM3:] + (
            d[0:NUM5] + (d[NUM5:2 * NUM5] + e[0:NUM5]) + (d[2 * NUM5:3 * NUM5] + e[NUM5:])
        )

    count = jnp.int32(0)
    for j in range(planes):
        count = count + steps_ref[j] * tiles_ref[j]

    def work(m, item):
        after = advance(item)
        weigh(after, buf_b)
        gather(item, buf_a, True)
        later = advance(after)
        weigh(later, buf_a)
        gather(after, buf_b, 2 * m + 1 < count)
        return later

    first = (jnp.int32(0), jnp.int32(0), jnp.int32(0))
    weigh(first, buf_a)
    lax.fori_loop(0, lax.shift_right_logical(count + 1, 1), work, first)

    def finish_plane(j, carry):
        def finish(tile, carry):
            slot = j * TILES + tile
            x = [spots[slot, n: n + 1, :] for n in range(3)]
            both = acc[slot, 0:NUM3, :] + acc[slot, NUM3:2 * NUM3, :]
            linear = both[18:24] + x[0] * both[0:6] + x[1] * both[6:12] + x[2] * both[12:18]
            second = acc[slot, 2 * NUM3:, :]
            v = [
                x[0] * second[n: n + 1] + x[1] * second[3 + n: 4 + n] + x[2] * second[6 + n: 7 + n]
                for n in range(3)
            ]
            scale = 0.5 * (
                second[0:1] + second[4:5] + second[8:9]
                + x[0] * second[9:10] + x[1] * second[10:11] + x[2] * second[11:12]
            )
            v = [v[n] + scale * x[n] for n in range(3)]
            bend = jnp.concatenate([x[a] * v[b] + x[b] * v[a] for a, b in PAIRS], axis=0)
            value = linear + bend
            value = jnp.concatenate([value, jnp.zeros((2, CAP), jnp.float32)], axis=0)
            at = starts_ref[jnp.maximum(j - 2, 0)] + CAP * tile
            low = jnp.bitwise_and(at, LANES - 1)
            place = pl.multiple_of(lax.shift_right_logical(at, 7) * 8, 8)
            keep = lane[0:8] >= low
            one = pltpu.roll(value[:, 0:LANES], low, 1)
            two = pltpu.roll(value[:, LANES:], low, 1)
            total[pl.ds(place, 8), :] += jnp.where(keep, one, 0.0)
            total[pl.ds(place + 8, 8), :] += jnp.where(keep, two, one)
            total[pl.ds(place + 16, 8), :] += jnp.where(keep, 0.0, two)
            return carry

        lax.fori_loop(0, tiles_ref[j], finish, 0)
        return carry

    lax.fori_loop(0, planes, finish_plane, 0)

    for i in range(cells):
        at = starts_ref[i]
        low = jnp.bitwise_and(at, LANES - 1)
        back = jnp.bitwise_and(LANES - low, LANES - 1)
        place = pl.multiple_of(lax.shift_right_logical(at, 7) * 8, 8)
        part = [pltpu.roll(total[pl.ds(place + 8 * n, 8), :], back, 1) for n in range(3)]
        keep = lane[0:8] < LANES - low
        out_ref[i, :, 0:LANES] = jnp.where(keep, part[0], part[1])
        out_ref[i, :, LANES:] = jnp.where(keep, part[1], part[2])


def near_call(before, sheet, after):
    planes = sheet.shape[0] // (3 * ROWS)
    cells = planes - 2
    vmem = pl.BlockSpec(memory_space=pltpu.VMEM)
    return pl.pallas_call(
        functools.partial(near_kernel, planes),
        out_shape=jax.ShapeDtypeStruct((cells, 8, CAP), jnp.float32),
        in_specs=[vmem, vmem, vmem],
        out_specs=vmem,
        scratch_shapes=[
            pltpu.VMEM((planes * BLOCKS * 16, LANES), jnp.float32),
            pltpu.VMEM((planes * BLOCKS * NUM, LANES), jnp.float32),
            pltpu.VMEM((planes * BLOCKS * 32, LANES), jnp.float32),
            pltpu.VMEM((planes * CHUNKS, 48, CAP), jnp.bfloat16),
            pltpu.VMEM((planes * CHUNKS, 128, CAP), jnp.bfloat16),
            pltpu.VMEM((planes * CHUNKS, CAP, 32), jnp.bfloat16),
            pltpu.VMEM((planes * TILES, 32, CAP), jnp.bfloat16),
            pltpu.VMEM((planes * TILES, 8, CAP), jnp.float32),
            pltpu.VMEM((planes * TILES, 32, CAP), jnp.float32),
            pltpu.VMEM((4, CAP, CAP), jnp.bfloat16),
            pltpu.VMEM((4, CAP, CAP), jnp.bfloat16),
            pltpu.VMEM((planes * TILES + 1, NUM, CAP), jnp.float32),
            pltpu.VMEM((10 * 16, LANES), jnp.float32),
            pltpu.VMEM((10 * 8, LANES), jnp.float32),
            pltpu.SMEM((planes,), jnp.int32),
            pltpu.SMEM((cells + 1,), jnp.int32),
            pltpu.SMEM((planes,), jnp.int32),
        ],
        compiler_params=pltpu.CompilerParams(vmem_limit_bytes=40 * 1024 * 1024),
        cost_estimate=pl.CostEstimate(flops=3 * 10**10, bytes_accessed=10**7, transcendentals=0),
        name="near",
    )(before, sheet, after)


def far_kernel(planes, spans, place_ref, moment_ref, applied_ref, sheet_ref, total, out_ref):
    cells = planes - 2
    span_x, span_y, span_z = spans
    shape = (span_z, LANES)
    half = LANES // 2
    column = lax.broadcasted_iota(jnp.int32, shape, 1)
    moment = []
    for m in range(9):
        value = moment_ref[:, 0, m // 2 * LANES: (m // 2 + 1) * LANES]
        if m % 2:
            value = pltpu.roll(value, half, 1)
        moment.append(jnp.where(column < half, value, 0.0))
    device = column // cells
    source = (
        (device // span_y * cells + column % cells).astype(jnp.float32),
        (device % span_y).astype(jnp.float32),
        lax.broadcasted_iota(jnp.int32, shape, 0).astype(jnp.float32),
    )
    w = (moment[5] - moment[7], moment[6] - moment[2], moment[1] - moment[3])
    index = {}
    for n, (a, b) in enumerate(PAIRS):
        index[a, b] = index[b, a] = n
    for i in range(cells):
        mine = (place_ref[0] * cells + i, place_ref[1], place_ref[2])
        r = [mine[n].astype(jnp.float32) - source[n] for n in range(3)]
        reach = jnp.maximum(jnp.maximum(jnp.abs(r[0]), jnp.abs(r[1])), jnp.abs(r[2]))
        inv = lax.rsqrt(r[0] * r[0] + r[1] * r[1] + r[2] * r[2] + CORE_SQUARE)
        inv = jnp.where(reach > 1.5, inv, 0.0)
        cube = inv * inv * inv
        fifth = cube * inv * inv
        radial = 2.0 * cube + KAPPA * fifth
        along = w[0] * r[0] + w[1] * r[1] + w[2] * r[2]
        turn = [cross(r, (moment[n], moment[3 + n], moment[6 + n])) for n in range(3)]
        slope = (3.0 * SECOND) * along * fifth
        cut = SECOND * cube
        bulk = SECOND * along * (radial - cube)
        front = -FIRST * radial
        stress = []
        for n, (a, b) in enumerate(PAIRS):
            element = (
                front * (turn[b][a] + turn[a][b])
                + slope * r[a] * r[b]
                - cut * (w[a] * r[b] + w[b] * r[a])
            )
            if a == b:
                element = element + bulk
            stress.append(
                jnp.sum(element, axis=(0, 1), keepdims=True)
                + 0.5 * (applied_ref[a, b] + applied_ref[b, a])
                + total[i, n: n + 1, :]
            )
        row = ROWS * (planes + 1 + i)
        t = [sheet_ref[row + 3 + n: row + 4 + n, :] for n in range(3)]
        b = [sheet_ref[row + 6 + n: row + 7 + n, :] for n in range(3)]
        force = [plus([stress[index[m, n]] * b[n] for n in range(3)]) for m in range(3)]
        for n, value in enumerate(cross(force, t)):
            out_ref[n, i, 0, :, :] = value


def pack_kernel(counts_ref, offset_ref, vector_ref, burgers_ref, all_ref, hold, sems):
    cells = offset_ref.shape[1]
    copies = [
        pltpu.make_async_copy(ref, hold.at[n], sems.at[n])
        for n, ref in enumerate((offset_ref, vector_ref, burgers_ref))
    ]
    for copy in copies:
        copy.start()
    slot = lax.broadcasted_iota(jnp.int32, (cells, CAP), 1)
    cell = lax.broadcasted_iota(jnp.int32, (cells, CAP), 0)
    live = jnp.zeros((cells, CAP), jnp.int32)
    for i in range(cells):
        live = jnp.where(cell == i, counts_ref[i], live)
    filled = slot < live
    for copy in copies:
        copy.wait()
    flat = [hold[n].reshape(3, cells, CAP) for n in range(3)]
    offset = [flat[0][n] for n in range(3)]
    tangent = [jnp.where(filled, flat[1][n], 0.0) for n in range(3)]
    charge = [jnp.where(filled, flat[2][n], 0.0) for n in range(3)]
    level = live.astype(jnp.float32)
    for m in range(3):
        for k in range(3):
            value = jnp.sum(charge[m] * tangent[k], axis=1, keepdims=True)
            level = jnp.where(slot == LANES + 3 * m + k, value, level)
    rows = offset + tangent + charge + [level]
    packed = jnp.concatenate([v[i: i + 1] for i in range(cells) for v in rows], axis=0)
    for d in range(all_ref.shape[0]):
        all_ref[d] = packed


def pick_kernel(planes, spans, place_ref, all_ref, sheet_ref, moment_ref):
    span_x, span_y, span_z = spans
    cells = planes - 2
    for dy in range(3):
        y = place_ref[1] + (dy - 1)
        for j in range(planes):
            step = (j + cells - 1) // cells - 1
            c = (j - 1) % cells
            x = place_ref[0] + step
            inside = (x >= 0) & (x < span_x) & (y >= 0) & (y < span_y)
            device = jnp.clip(x, 0, span_x - 1) * span_y + jnp.clip(y, 0, span_y - 1)
            row = ROWS * (dy * planes + j)
            sheet_ref[row: row + ROWS, :] = jnp.where(
                inside, all_ref[device, ROWS * c: ROWS * c + ROWS, :], 0.0
            )
    rows = [
        all_ref[d, ROWS * c + ROWS - 1: ROWS * c + ROWS, LANES:]
        for d in range(span_x * span_y)
        for c in range(cells)
    ]
    rows.append(jnp.zeros((LANES - len(rows), LANES), jnp.float32))
    flip = jnp.transpose(jnp.concatenate(rows, axis=0))
    half = LANES // 2
    line = [
        flip[2 * r: 2 * r + 1] + pltpu.roll(flip[2 * r + 1: 2 * r + 2], half, 1) for r in range(5)
    ]
    line = jnp.concatenate(line, axis=1)
    moment_ref[...] = jnp.broadcast_to(line[None], moment_ref.shape)


def beside(first, last, axis):
    devices = lax.axis_size(axis)
    up = [(i, i + 1) for i in range(devices - 1)]
    down = [(i + 1, i) for i in range(devices - 1)]
    return lax.ppermute(last, axis, up), lax.ppermute(first, axis, down)


def local(seg_offset, seg_vector, burgers, cell_counts, applied):
    cells = seg_offset.shape[1]
    planes = cells + 2
    spans = tuple(lax.axis_size(a) for a in ("gx", "gy", "gz"))
    place = jnp.stack([lax.axis_index(a) for a in ("gx", "gy", "gz")]).astype(jnp.int32)
    devices = spans[0] * spans[1]
    vmem = pl.BlockSpec(memory_space=pltpu.VMEM)
    smem = pl.BlockSpec(memory_space=pltpu.SMEM)
    anywhere = pl.BlockSpec(memory_space=pl.ANY)
    limit = pltpu.CompilerParams(vmem_limit_bytes=40 * 1024 * 1024)
    packed = pl.pallas_call(
        pack_kernel,
        out_shape=jax.ShapeDtypeStruct((devices, cells * ROWS, CAP), jnp.float32),
        in_specs=[smem] + [anywhere] * 3,
        out_specs=vmem,
        scratch_shapes=[
            pltpu.VMEM((3,) + seg_offset.shape, jnp.float32),
            pltpu.SemaphoreType.DMA((3,)),
        ],
        compiler_params=pltpu.CompilerParams(vmem_limit_bytes=60 * 1024 * 1024),
        name="pack",
    )(cell_counts.reshape(cells), seg_offset, seg_vector, burgers)
    every = lax.all_to_all(packed, ("gx", "gy"), 0, 0)
    sheet, moments = pl.pallas_call(
        functools.partial(pick_kernel, planes, spans),
        out_shape=(
            jax.ShapeDtypeStruct((3 * planes * ROWS, CAP), jnp.float32),
            jax.ShapeDtypeStruct((spans[2], 1, 5 * LANES), jnp.float32),
        ),
        in_specs=[smem, vmem],
        out_specs=(vmem, vmem),
        compiler_params=limit,
        name="pick",
    )(place, every)
    before, after = beside(sheet, sheet, "gz")
    moments = lax.all_to_all(moments, "gz", 0, 0)
    total = near_call(before, sheet, after)
    return pl.pallas_call(
        functools.partial(far_kernel, planes, spans),
        out_shape=jax.ShapeDtypeStruct(seg_offset.shape, jnp.float32),
        in_specs=[smem, vmem, smem, vmem, vmem],
        out_specs=vmem,
        compiler_params=limit,
        name="far",
    )(place, moments, applied, sheet, total)


def solution(mesh):
    placed = P(None, "gx", "gy", "gz", None)
    return jax.shard_map(
        local,
        mesh=mesh,
        in_specs=(placed, placed, placed, P("gx", "gy", "gz"), P()),
        out_specs=placed,
        check_vma=False,
    )
```

```python
import functools
import math

import jax
import jax.numpy as jnp
from jax import lax
from jax.experimental import pallas as pl
from jax.experimental.pallas import tpu as pltpu
from jax.sharding import PartitionSpec as P

CORE_SQUARE = 0.2 * 0.2
FIRST = 1.0 / (8.0 * math.pi)
SECOND = 1.0 / (4.0 * math.pi * 0.7)
KAPPA = 3.0 * CORE_SQUARE
CAP = 256
LANES = 128
ROWS = 10
PAIRS = ((0, 0), (0, 1), (0, 2), (1, 1), (1, 2), (2, 2))
NUM3 = 24
NUM5 = 40
NUM = NUM3 + NUM5
BLOCKS = 24
CHUNKS = 10
TILES = 3


def cross(a, b):
    return (
        a[1] * b[2] - a[2] * b[1],
        a[2] * b[0] - a[0] * b[2],
        a[0] * b[1] - a[1] * b[0],
    )


def plus(terms):
    terms = [t for t in terms if t is not None]
    total = terms[0]
    for t in terms[1:]:
        total = total + t
    return total


def features(y, t, b):
    w = cross(b, t)
    turn = [[None, b[2], -b[1]], [-b[2], None, b[0]], [b[1], -b[0], None]]
    c2w = [SECOND * v for v in w]
    lin3, lin5 = {}, {}
    for n, (i, j) in enumerate(PAIRS):
        for m in range(3):
            parts = []
            if turn[i][m] is not None:
                parts.append(turn[i][m] * t[j])
            if turn[j][m] is not None:
                parts.append(turn[j][m] * t[i])
            base = plus(parts) * (-FIRST) if parts else None
            a3 = [2.0 * base] if base is not None else []
            a5 = [base] if base is not None else []
            if i == j:
                a3.append(c2w[m])
                a5.append(c2w[m])
            if m == j:
                a3.append(-c2w[i])
            if m == i:
                a3.append(-c2w[j])
            lin3[m, n] = plus(a3) if a3 else None
            lin5[m, n] = KAPPA * plus(a5) if a5 else None
    w3 = [3.0 * v for v in c2w]
    wy = [[w3[m] * y[n] for n in range(3)] for m in range(3)]
    dot = wy[0][0] + wy[1][1] + wy[2][2]
    doty = [dot * y[n] for n in range(3)]
    rows3, rows5 = {}, {}
    for n, (i, j) in enumerate(PAIRS):
        zero3, zero5 = [], [doty[i] * y[j]]
        for m in range(3):
            if lin3[m, n] is not None:
                rows3[6 * m + n] = lin3[m, n]
                zero3.append(lin3[m, n] * y[m])
            quad = [wy[m][i] * y[j]]
            if m == i:
                quad.append(doty[j])
            if m == j:
                quad.append(doty[i])
            if lin5[m, n] is not None:
                quad.append(lin5[m, n])
                zero5.append(lin5[m, n] * y[m])
            rows5[6 * m + n] = plus(quad)
        if zero3:
            rows3[18 + n] = -plus(zero3)
        rows5[18 + n] = -plus(zero5)
    for m in range(3):
        for n in range(3):
            rows5[24 + 3 * m + n] = -wy[m][n]
        rows5[33 + m] = w3[m]
    return rows3, rows5


def halves(value, terms):
    out = []
    for k in range(terms):
        part = value.astype(jnp.bfloat16)
        out.append(part)
        if k + 1 < terms:
            value = value - part.astype(jnp.float32)
    return out


def near_kernel(
    planes, before_ref, middle_ref, after_ref, out_ref,
    raw, feat, cols, left3, left5, left_d, right_d, spots, line, buf_a, buf_b, acc, aim, total, steps_ref, starts_ref, tiles_ref,
):
    sources = (before_ref, middle_ref, after_ref)
    cells = planes - 2
    columns = [(k, c) for k in range(3) for c in range(3)]
    lane = lax.broadcasted_iota(jnp.int32, (16, LANES), 1)
    lift = lax.broadcasted_iota(jnp.int32, (16, LANES), 0)
    mm = functools.partial(jnp.dot, preferred_element_type=jnp.float32)
    for ref in (raw, aim, total, line):
        ref[...] = jnp.zeros_like(ref)

    def append(ref, first, second, at, offset):
        rows = first.shape[0]
        low = jnp.bitwise_and(at, LANES - 1)
        base = lax.shift_right_logical(at, 7) + offset
        first = pltpu.roll(first, low, 1)
        second = pltpu.roll(second, low, 1)
        keep = lane[0:rows] >= low
        place = pl.multiple_of(base * 16, 16)
        ref[pl.ds(place, rows), :] = jnp.where(keep, first, ref[pl.ds(place, rows), :])
        ref[pl.ds(place + 16, rows), :] = jnp.where(keep, second, first)
        ref[pl.ds(place + 32, rows), :] = jnp.where(keep, 0.0, second)

    goal = jnp.int32(0)
    for j in range(planes):
        at = jnp.int32(0)
        for k, c in columns:
            row = ROWS * (c * planes + j)
            first = sources[k][row: row + ROWS, 0:LANES]
            second = sources[k][row: row + ROWS, LANES:]
            count = first[ROWS - 1: ROWS, 0:1].astype(jnp.int32)[0, 0]
            if k == 1 and c == 1 and 0 < j < planes - 1:
                shift = jnp.where(lift[0:8] == 0, j - 0.5, -0.5)
                mark = lift[0:8] < 3
                starts_ref[j - 1] = goal
                append(
                    aim,
                    jnp.where(mark, first[0:8] + shift, float(j)),
                    jnp.where(mark, second[0:8] + shift, float(j)),
                    goal,
                    0,
                )
                goal = goal + count
            shift = (
                jnp.where(lift < 3, -0.5, 0.0)
                + jnp.where(lift == 1, float(c - 1), 0.0)
                + jnp.where(lift == 2, float(k - 1), 0.0)
            )[0:ROWS]
            append(raw, first + shift, second + shift, at, j * BLOCKS)
            at = at + count
        steps_ref[j] = jnp.maximum(lax.shift_right_logical(at + CAP - 1, 8), 1)
    starts_ref[cells] = goal
    for j in range(planes):
        reach = starts_ref[min(j, cells - 1) + 1] - starts_ref[max(j - 2, 0)]
        tiles_ref[j] = lax.shift_right_logical(reach + CAP - 1, 8)

    for j in range(planes):
        for tile in range(min(j, cells - 1) + 1 - max(j - 2, 0)):
            at = starts_ref[max(j - 2, 0)] + CAP * tile
            at = jnp.minimum(at, starts_ref[cells])
            low = jnp.bitwise_and(at, LANES - 1)
            back = jnp.bitwise_and(LANES - low, LANES - 1)
            place = pl.multiple_of(lax.shift_right_logical(at, 7) * 16, 16)
            part = [pltpu.roll(aim[pl.ds(place + 16 * n, 8), :], back, 1) for n in range(3)]
            keep = lane[0:8] < LANES - low
            spot = jnp.concatenate(
                [jnp.where(keep, part[0], part[1]), jnp.where(keep, part[1], part[2])], axis=1
            )
            x = [spot[0:1] - float(j), spot[1:2], spot[2:3]]
            size = x[0] * x[0] + x[1] * x[1] + x[2] * x[2]
            size = jnp.where(jnp.abs(spot[3:4] - float(j)) < 1.5, size, 1e30)
            slot = j * TILES + tile
            for n in range(3):
                spots[slot, n: n + 1, :] = x[n]
                part = [v.astype(jnp.float32) for v in halves(-2.0 * x[n], 3)]
                for r, p in enumerate((0, 1, 0, 1, 2, 0)):
                    line[slot, 6 * n + r: 6 * n + r + 1, :] = part[p]
            line[slot, 18:21, :] = jnp.ones((3, CAP), jnp.float32)
            for r, p in enumerate(halves(size, 3)):
                line[slot, 21 + r: 22 + r, :] = p.astype(jnp.float32)
            right_d[slot] = line[slot].astype(jnp.bfloat16)

    def describe(j, g):
        start = (j * BLOCKS + g * 8) * 16
        row = jnp.swapaxes(jnp.stack([raw[start + 16 * q: start + 16 * q + 8, :] for q in range(8)]), 0, 1)
        row = [row[r] for r in range(8)] + [raw[pl.ds(start + 8, 8, stride=16), :]]
        rows3, rows5 = features(row[0:3], row[3:6], row[6:9])
        base = (j * BLOCKS + g * 8) * NUM
        def spread(ref, first, step, rows):
            for k in range(0, len(rows), 8):
                part = jnp.swapaxes(jnp.stack(rows[k: k + 8]), 0, 1)
                for q in range(8):
                    ref[first + q * step + k: first + q * step + k + 8, :] = part[q]

        none = jnp.zeros((8, LANES), jnp.float32)
        spread(feat, base, NUM, [rows3.get(r, none) for r in range(NUM3)] + [rows5.get(r, none) for r in range(NUM5)])
        y = row[0:3]
        size = y[0] * y[0] + y[1] * y[1] + (y[2] * y[2] + CORE_SQUARE)
        line_rows = []
        for n in range(3):
            part = [v.astype(jnp.float32) for v in halves(y[n], 3)]
            line_rows += [part[p] for p in (0, 0, 1, 1, 0, 2)]
        line_rows += [p.astype(jnp.float32) for p in halves(size, 3)]
        line_rows += [none + 1.0] * 3 + [none] * 8
        spread(cols, (j * BLOCKS + g * 8) * 32, 32, line_rows)

    for j in range(planes):
        describe(j, 0)
    for g in range(1, BLOCKS // 8):
        for j in range(planes):
            pl.when(steps_ref[j] > 4 * g)(functools.partial(describe, j, g))

    def rest(value):
        return value - value.astype(jnp.bfloat16).astype(jnp.float32)

    def split_body(n, state):
        j, c = state
        for part in range(2):
            index = j * CHUNKS + c + part
            for h in range(2):
                block = j * BLOCKS + 2 * (c + part) + h
                span = slice(h * LANES, (h + 1) * LANES)
                at = pl.multiple_of(block * NUM, 8)
                value = feat[pl.ds(at, NUM3), :]
                left3[index, :, span] = jnp.concatenate([value, rest(value)], axis=0).astype(
                    jnp.bfloat16
                )
                value = feat[pl.ds(at + NUM3, NUM5), :]
                second = rest(value)
                third = rest(second)
                left5[index, :, span] = jnp.concatenate(
                    [value, second, third, jnp.zeros((8, LANES), jnp.float32)], axis=0
                ).astype(jnp.bfloat16)
                turned = cols[pl.ds(pl.multiple_of(block * 32, 32), 32), :].astype(jnp.bfloat16)
                left_d[index, span, :] = jnp.transpose(turned)
        wrap = c + 2 >= steps_ref[j]
        return (
            jnp.where(wrap, jnp.minimum(j + 1, planes - 1), j),
            jnp.where(wrap, 0, c + 2),
        )

    pieces = jnp.int32(0)
    for j in range(planes):
        pieces = pieces + lax.shift_right_logical(steps_ref[j] + 1, 1)
    lax.fori_loop(0, pieces, split_body, (jnp.int32(0), jnp.int32(0)))

    def advance(item):
        j, tile, c = item
        wrap = c + 1 >= steps_ref[j]
        turn = wrap & (tile + 1 >= tiles_ref[j])
        end = turn & (j + 1 >= planes)
        new_j = jnp.where(turn, jnp.minimum(j + 1, planes - 1), j)
        new_tile = jnp.where(turn, 0, jnp.where(wrap, tile + 1, tile))
        new_c = jnp.where(wrap, 0, c + 1)
        return (new_j, jnp.where(end, tile, new_tile), jnp.where(end, c, new_c))

    def weigh(item, buf):
        j, tile, c = item
        apart = mm(left_d[j * CHUNKS + c], right_d[j * TILES + tile])
        for s in range(CAP // 16):
            span = slice(s * 16, (s + 1) * 16)
            inv = lax.rsqrt(apart[span, :])
            square = inv * inv
            cube = square * inv
            fifth = cube * square
            buf[0, span, :], buf[1, span, :] = halves(cube, 2)
            buf[2, span, :], buf[3, span, :] = halves(fifth, 2)

    def gather(item, buf, live):
        j, tile, c = item
        index = j * CHUNKS + c
        slot = jnp.where(live, j * TILES + tile, planes * TILES)
        a = mm(left3[index], buf[0])
        b = mm(left3[index, 0:32, :], buf[1])
        d = mm(left5[index], buf[2])
        e = mm(left5[index, 0:2 * NUM5, :], buf[3])
        old = jnp.where(c == 0, 0.0, acc[slot])
        acc[slot, 0:NUM3, :] = old[0:NUM3] + (a[0:NUM3] + (a[NUM3:] + b[0:NUM3]))
        acc[slot, NUM3:, :] = old[NUM3:] + (
            d[0:NUM5] + (d[NUM5:2 * NUM5] + e[0:NUM5]) + (d[2 * NUM5:3 * NUM5] + e[NUM5:])
        )

    count = jnp.int32(0)
    for j in range(planes):
        count = count + steps_ref[j] * tiles_ref[j]

    def work(m, item):
        after = advance(item)
        weigh(after, buf_b)
        gather(item, buf_a, True)
        later = advance(after)
        weigh(later, buf_a)
        gather(after, buf_b, 2 * m + 1 < count)
        return later

    first = (jnp.int32(0), jnp.int32(0), jnp.int32(0))
    weigh(first, buf_a)
    lax.fori_loop(0, lax.shift_right_logical(count + 1, 1), work, first)

    def finish(j, tile):
        slot = j * TILES + tile
        x = [spots[slot, n: n + 1, :] for n in range(3)]
        both = acc[slot, 0:NUM3, :] + acc[slot, NUM3:2 * NUM3, :]
        linear = both[18:24] + x[0] * both[0:6] + x[1] * both[6:12] + x[2] * both[12:18]
        second = acc[slot, 2 * NUM3:, :]
        v = [
            x[0] * second[n: n + 1] + x[1] * second[3 + n: 4 + n] + x[2] * second[6 + n: 7 + n]
            for n in range(3)
        ]
        scale = 0.5 * (
            second[0:1] + second[4:5] + second[8:9]
            + x[0] * second[9:10] + x[1] * second[10:11] + x[2] * second[11:12]
        )
        v = [v[n] + scale * x[n] for n in range(3)]
        bend = jnp.concatenate([x[a] * v[b] + x[b] * v[a] for a, b in PAIRS], axis=0)
        value = linear + bend
        value = jnp.concatenate([value, jnp.zeros((2, CAP), jnp.float32)], axis=0)
        at = starts_ref[max(j - 2, 0)] + CAP * tile
        low = jnp.bitwise_and(at, LANES - 1)
        place = pl.multiple_of(lax.shift_right_logical(at, 7) * 8, 8)
        keep = lane[0:8] >= low
        one = pltpu.roll(value[:, 0:LANES], low, 1)
        two = pltpu.roll(value[:, LANES:], low, 1)
        total[pl.ds(place, 8), :] += jnp.where(keep, one, 0.0)
        total[pl.ds(place + 8, 8), :] += jnp.where(keep, two, one)
        total[pl.ds(place + 16, 8), :] += jnp.where(keep, 0.0, two)

    for j in range(planes):
        finish(j, 0)
    for j in range(planes):
        for tile in range(1, min(j, cells - 1) + 1 - max(j - 2, 0)):
            pl.when(tile < tiles_ref[j])(functools.partial(finish, j, tile))

    for i in range(cells):
        at = starts_ref[i]
        low = jnp.bitwise_and(at, LANES - 1)
        back = jnp.bitwise_and(LANES - low, LANES - 1)
        place = pl.multiple_of(lax.shift_right_logical(at, 7) * 8, 8)
        part = [pltpu.roll(total[pl.ds(place + 8 * n, 8), :], back, 1) for n in range(3)]
        keep = lane[0:8] < LANES - low
        out_ref[i, :, 0:LANES] = jnp.where(keep, part[0], part[1])
        out_ref[i, :, LANES:] = jnp.where(keep, part[1], part[2])


def near_call(before, sheet, after):
    planes = sheet.shape[0] // (3 * ROWS)
    cells = planes - 2
    vmem = pl.BlockSpec(memory_space=pltpu.VMEM)
    return pl.pallas_call(
        functools.partial(near_kernel, planes),
        out_shape=jax.ShapeDtypeStruct((cells, 8, CAP), jnp.float32),
        in_specs=[vmem, vmem, vmem],
        out_specs=vmem,
        scratch_shapes=[
            pltpu.VMEM((planes * BLOCKS * 16, LANES), jnp.float32),
            pltpu.VMEM((planes * BLOCKS * NUM, LANES), jnp.float32),
            pltpu.VMEM((planes * BLOCKS * 32, LANES), jnp.float32),
            pltpu.VMEM((planes * CHUNKS, 48, CAP), jnp.bfloat16),
            pltpu.VMEM((planes * CHUNKS, 128, CAP), jnp.bfloat16),
            pltpu.VMEM((planes * CHUNKS, CAP, 32), jnp.bfloat16),
            pltpu.VMEM((planes * TILES, 32, CAP), jnp.bfloat16),
            pltpu.VMEM((planes * TILES, 8, CAP), jnp.float32),
            pltpu.VMEM((planes * TILES, 32, CAP), jnp.float32),
            pltpu.VMEM((4, CAP, CAP), jnp.bfloat16),
            pltpu.VMEM((4, CAP, CAP), jnp.bfloat16),
            pltpu.VMEM((planes * TILES + 1, NUM, CAP), jnp.float32),
            pltpu.VMEM((10 * 16, LANES), jnp.float32),
            pltpu.VMEM((10 * 8, LANES), jnp.float32),
            pltpu.SMEM((planes,), jnp.int32),
            pltpu.SMEM((cells + 1,), jnp.int32),
            pltpu.SMEM((planes,), jnp.int32),
        ],
        compiler_params=pltpu.CompilerParams(vmem_limit_bytes=40 * 1024 * 1024),
        cost_estimate=pl.CostEstimate(flops=3 * 10**10, bytes_accessed=10**7, transcendentals=0),
        name="near",
    )(before, sheet, after)


def far_kernel(planes, spans, moment_ref, applied_ref, sheet_ref, total, out_ref):
    cells = planes - 2
    span_x, span_y, span_z = spans
    shape = (span_z, LANES)
    half = LANES // 2
    column = lax.broadcasted_iota(jnp.int32, shape, 1)
    moment = []
    for m in range(9):
        value = moment_ref[:, 0, m // 2 * LANES: (m // 2 + 1) * LANES]
        if m % 2:
            value = pltpu.roll(value, half, 1)
        moment.append(jnp.where(column < half, value, 0.0))
    device = column // cells
    source = (
        (device // span_y * cells + column % cells).astype(jnp.float32),
        (device % span_y).astype(jnp.float32),
        lax.broadcasted_iota(jnp.int32, shape, 0).astype(jnp.float32),
    )
    w = (moment[5] - moment[7], moment[6] - moment[2], moment[1] - moment[3])
    index = {}
    for n, (a, b) in enumerate(PAIRS):
        index[a, b] = index[b, a] = n
    pieces = []
    for i in range(cells):
        mine = (lax.axis_index("gx") * cells + i, lax.axis_index("gy"), lax.axis_index("gz"))
        r = [mine[n].astype(jnp.float32) - source[n] for n in range(3)]
        reach = jnp.maximum(jnp.maximum(jnp.abs(r[0]), jnp.abs(r[1])), jnp.abs(r[2]))
        inv = lax.rsqrt(r[0] * r[0] + r[1] * r[1] + r[2] * r[2] + CORE_SQUARE)
        inv = jnp.where(reach > 1.5, inv, 0.0)
        cube = inv * inv * inv
        fifth = cube * inv * inv
        radial = 2.0 * cube + KAPPA * fifth
        along = w[0] * r[0] + w[1] * r[1] + w[2] * r[2]
        turn = [cross(r, (moment[n], moment[3 + n], moment[6 + n])) for n in range(3)]
        slope = (3.0 * SECOND) * along * fifth
        cut = SECOND * cube
        bulk = SECOND * along * (radial - cube)
        front = -FIRST * radial
        for n, (a, b) in enumerate(PAIRS):
            element = (
                front * (turn[b][a] + turn[a][b])
                + slope * r[a] * r[b]
                - cut * (w[a] * r[b] + w[b] * r[a])
            )
            if a == b:
                element = element + bulk
            pieces.append(plus([element[k: k + 8] for k in range(0, span_z, 8)]))
    pieces = [
        jnp.sum(jnp.sum(jnp.swapaxes(jnp.stack(pieces[k: k + 8]), 0, 1), axis=0), axis=1, keepdims=True)
        for k in range(0, len(pieces), 8)
    ]
    for i in range(cells):
        stress = []
        for n, (a, b) in enumerate(PAIRS):
            k = 6 * i + n
            stress.append(
                pieces[k // 8][k % 8: k % 8 + 1]
                + 0.5 * (applied_ref[a: a + 1, b: b + 1] + applied_ref[b: b + 1, a: a + 1])
                + total[i, n: n + 1, :]
            )
        row = ROWS * (planes + 1 + i)
        t = [sheet_ref[row + 3 + n: row + 4 + n, :] for n in range(3)]
        b = [sheet_ref[row + 6 + n: row + 7 + n, :] for n in range(3)]
        force = [plus([stress[index[m, n]] * b[n] for n in range(3)]) for m in range(3)]
        for n, value in enumerate(cross(force, t)):
            out_ref[n, i, 0, :, :] = value


def pack_kernel(counts_ref, offset_ref, vector_ref, burgers_ref, all_ref, hold, count_hold, sems):
    cells = offset_ref.shape[1]
    copies = [
        pltpu.make_async_copy(ref, hold.at[n], sems.at[n])
        for n, ref in enumerate((offset_ref, vector_ref, burgers_ref))
    ]
    number = pltpu.make_async_copy(counts_ref, count_hold, sems.at[3])
    number.start()
    for copy in copies:
        copy.start()
    number.wait()
    slot = lax.broadcasted_iota(jnp.int32, (cells, CAP), 1)
    cell = lax.broadcasted_iota(jnp.int32, (cells, CAP), 0)
    live = jnp.zeros((cells, CAP), jnp.int32)
    for i in range(cells):
        live = jnp.where(cell == i, count_hold[i], live)
    filled = slot < live
    for copy in copies:
        copy.wait()
    flat = [hold[n].reshape(3, cells, CAP) for n in range(3)]
    offset = [flat[0][n] for n in range(3)]
    tangent = [jnp.where(filled, flat[1][n], 0.0) for n in range(3)]
    charge = [jnp.where(filled, flat[2][n], 0.0) for n in range(3)]
    level = live.astype(jnp.float32)
    for m in range(3):
        for k in range(3):
            value = jnp.sum(charge[m] * tangent[k], axis=1, keepdims=True)
            level = jnp.where(slot == LANES + 3 * m + k, value, level)
    rows = offset + tangent + charge + [level]
    packed = jnp.concatenate([v[i: i + 1] for i in range(cells) for v in rows], axis=0)
    for d in range(all_ref.shape[0]):
        all_ref[d] = packed


def pick_kernel(planes, spans, all_ref, sheet_ref, moment_ref):
    span_x, span_y, span_z = spans
    cells = planes - 2
    for dy in range(3):
        y = lax.axis_index("gy") + (dy - 1)
        for j in range(planes):
            step = (j + cells - 1) // cells - 1
            c = (j - 1) % cells
            x = lax.axis_index("gx") + step
            inside = (x >= 0) & (x < span_x) & (y >= 0) & (y < span_y)
            device = jnp.clip(x, 0, span_x - 1) * span_y + jnp.clip(y, 0, span_y - 1)
            row = ROWS * (dy * planes + j)
            sheet_ref[row: row + ROWS, :] = jnp.where(
                inside, all_ref[device, ROWS * c: ROWS * c + ROWS, :], 0.0
            )
    rows = [
        all_ref[d, ROWS * c + ROWS - 1: ROWS * c + ROWS, LANES:]
        for d in range(span_x * span_y)
        for c in range(cells)
    ]
    rows.append(jnp.zeros((LANES - len(rows), LANES), jnp.float32))
    flip = jnp.transpose(jnp.concatenate(rows, axis=0))
    half = LANES // 2
    line = [
        flip[2 * r: 2 * r + 1] + pltpu.roll(flip[2 * r + 1: 2 * r + 2], half, 1) for r in range(5)
    ]
    line = jnp.concatenate(line, axis=1)
    moment_ref[...] = jnp.broadcast_to(line[None], moment_ref.shape)


def beside(first, last, axis):
    devices = lax.axis_size(axis)
    up = [(i, i + 1) for i in range(devices - 1)]
    down = [(i + 1, i) for i in range(devices - 1)]
    return lax.ppermute(last, axis, up), lax.ppermute(first, axis, down)


def local(seg_offset, seg_vector, burgers, cell_counts, applied):
    cells = seg_offset.shape[1]
    planes = cells + 2
    spans = tuple(lax.axis_size(a) for a in ("gx", "gy", "gz"))
    devices = spans[0] * spans[1]
    vmem = pl.BlockSpec(memory_space=pltpu.VMEM)
    anywhere = pl.BlockSpec(memory_space=pl.ANY)
    limit = pltpu.CompilerParams(vmem_limit_bytes=40 * 1024 * 1024)
    packed = pl.pallas_call(
        pack_kernel,
        out_shape=jax.ShapeDtypeStruct((devices, cells * ROWS, CAP), jnp.float32),
        in_specs=[anywhere] * 4,
        out_specs=vmem,
        scratch_shapes=[
            pltpu.VMEM((3,) + seg_offset.shape, jnp.float32),
            pltpu.SMEM((cells,), jnp.int32),
            pltpu.SemaphoreType.DMA((4,)),
        ],
        compiler_params=pltpu.CompilerParams(vmem_limit_bytes=60 * 1024 * 1024),
        name="pack",
    )(cell_counts.reshape(cells), seg_offset, seg_vector, burgers)
    every = lax.all_to_all(packed, ("gx", "gy"), 0, 0)
    sheet, moments = pl.pallas_call(
        functools.partial(pick_kernel, planes, spans),
        out_shape=(
            jax.ShapeDtypeStruct((3 * planes * ROWS, CAP), jnp.float32),
            jax.ShapeDtypeStruct((spans[2], 1, 5 * LANES), jnp.float32),
        ),
        in_specs=[vmem],
        out_specs=(vmem, vmem),
        compiler_params=limit,
        name="pick",
    )(every)
    before, after = beside(sheet, sheet, "gz")
    moments = lax.all_to_all(moments, "gz", 0, 0)
    total = near_call(before, sheet, after)
    return pl.pallas_call(
        functools.partial(far_kernel, planes, spans),
        out_shape=jax.ShapeDtypeStruct(seg_offset.shape, jnp.float32),
        in_specs=[vmem] * 4,
        out_specs=vmem,
        compiler_params=limit,
        name="far",
    )(moments, applied, sheet, total)


def solution(mesh):
    placed = P(None, "gx", "gy", "gz", None)
    return jax.shard_map(
        local,
        mesh=mesh,
        in_specs=(placed, placed, placed, P("gx", "gy", "gz"), P()),
        out_specs=placed,
        check_vma=False,
    )
```

```python
import functools
import math

import jax
import jax.numpy as jnp
from jax import lax
from jax.experimental import pallas as pl
from jax.experimental.pallas import tpu as pltpu
from jax.sharding import PartitionSpec as P

CORE_SQUARE = 0.2 * 0.2
FIRST = 1.0 / (8.0 * math.pi)
SECOND = 1.0 / (4.0 * math.pi * 0.7)
KAPPA = 3.0 * CORE_SQUARE
CAP = 256
LANES = 128
ROWS = 10
PAIRS = ((0, 0), (0, 1), (0, 2), (1, 1), (1, 2), (2, 2))
NUM3 = 24
NUM5 = 40
NUM = NUM3 + NUM5
BLOCKS = 24
CHUNKS = 10
TILES = 3


def cross(a, b):
    return (
        a[1] * b[2] - a[2] * b[1],
        a[2] * b[0] - a[0] * b[2],
        a[0] * b[1] - a[1] * b[0],
    )


def plus(terms):
    terms = [t for t in terms if t is not None]
    total = terms[0]
    for t in terms[1:]:
        total = total + t
    return total


def features(y, t, b):
    w = cross(b, t)
    turn = [[None, b[2], -b[1]], [-b[2], None, b[0]], [b[1], -b[0], None]]
    c2w = [SECOND * v for v in w]
    lin3, lin5 = {}, {}
    for n, (i, j) in enumerate(PAIRS):
        for m in range(3):
            parts = []
            if turn[i][m] is not None:
                parts.append(turn[i][m] * t[j])
            if turn[j][m] is not None:
                parts.append(turn[j][m] * t[i])
            base = plus(parts) * (-FIRST) if parts else None
            a3 = [2.0 * base] if base is not None else []
            a5 = [base] if base is not None else []
            if i == j:
                a3.append(c2w[m])
                a5.append(c2w[m])
            if m == j:
                a3.append(-c2w[i])
            if m == i:
                a3.append(-c2w[j])
            lin3[m, n] = plus(a3) if a3 else None
            lin5[m, n] = KAPPA * plus(a5) if a5 else None
    w3 = [3.0 * v for v in c2w]
    wy = [[w3[m] * y[n] for n in range(3)] for m in range(3)]
    dot = wy[0][0] + wy[1][1] + wy[2][2]
    doty = [dot * y[n] for n in range(3)]
    rows3, rows5 = {}, {}
    for n, (i, j) in enumerate(PAIRS):
        zero3, zero5 = [], [doty[i] * y[j]]
        for m in range(3):
            if lin3[m, n] is not None:
                rows3[6 * m + n] = lin3[m, n]
                zero3.append(lin3[m, n] * y[m])
            quad = [wy[m][i] * y[j]]
            if m == i:
                quad.append(doty[j])
            if m == j:
                quad.append(doty[i])
            if lin5[m, n] is not None:
                quad.append(lin5[m, n])
                zero5.append(lin5[m, n] * y[m])
            rows5[6 * m + n] = plus(quad)
        if zero3:
            rows3[18 + n] = -plus(zero3)
        rows5[18 + n] = -plus(zero5)
    for m in range(3):
        for n in range(3):
            rows5[24 + 3 * m + n] = -wy[m][n]
        rows5[33 + m] = w3[m]
    return rows3, rows5


def halves(value, terms):
    out = []
    for k in range(terms):
        part = value.astype(jnp.bfloat16)
        out.append(part)
        if k + 1 < terms:
            value = value - part.astype(jnp.float32)
    return out


def near_kernel(
    planes, before_ref, middle_ref, after_ref, out_ref,
    raw, feat, cols, left3, left5, left_d, right_d, spots, line, buf_a, buf_b, acc, aim, total, steps_ref, starts_ref, tiles_ref,
):
    sources = (before_ref, middle_ref, after_ref)
    cells = planes - 2
    columns = [(k, c) for k in range(3) for c in range(3)]
    lane = lax.broadcasted_iota(jnp.int32, (16, LANES), 1)
    lift = lax.broadcasted_iota(jnp.int32, (16, LANES), 0)
    mm = functools.partial(jnp.dot, preferred_element_type=jnp.float32)
    for ref in (raw, aim, total, line):
        ref[...] = jnp.zeros_like(ref)

    def append(ref, first, second, at, offset):
        rows = first.shape[0]
        low = jnp.bitwise_and(at, LANES - 1)
        base = lax.shift_right_logical(at, 7) + offset
        first = pltpu.roll(first, low, 1)
        second = pltpu.roll(second, low, 1)
        keep = lane[0:rows] >= low
        place = pl.multiple_of(base * 16, 16)
        ref[pl.ds(place, rows), :] = jnp.where(keep, first, ref[pl.ds(place, rows), :])
        ref[pl.ds(place + 16, rows), :] = jnp.where(keep, second, first)
        ref[pl.ds(place + 32, rows), :] = jnp.where(keep, 0.0, second)

    goal = jnp.int32(0)
    for j in range(planes):
        at = jnp.int32(0)
        for k, c in columns:
            row = ROWS * (c * planes + j)
            first = sources[k][row: row + ROWS, 0:LANES]
            second = sources[k][row: row + ROWS, LANES:]
            count = first[ROWS - 1: ROWS, 0:1].astype(jnp.int32)[0, 0]
            if k == 0:
                count = jnp.where(lax.axis_index("gz") == 0, 0, count)
            if k == 1 and c == 1 and 0 < j < planes - 1:
                shift = jnp.where(lift[0:8] == 0, j - 0.5, -0.5)
                mark = lift[0:8] < 3
                starts_ref[j - 1] = goal
                append(
                    aim,
                    jnp.where(mark, first[0:8] + shift, float(j)),
                    jnp.where(mark, second[0:8] + shift, float(j)),
                    goal,
                    0,
                )
                goal = goal + count
            shift = (
                jnp.where(lift < 3, -0.5, 0.0)
                + jnp.where(lift == 1, float(c - 1), 0.0)
                + jnp.where(lift == 2, float(k - 1), 0.0)
            )[0:ROWS]
            append(raw, first + shift, second + shift, at, j * BLOCKS)
            at = at + count
        steps_ref[j] = jnp.maximum(lax.shift_right_logical(at + CAP - 1, 8), 1)
    starts_ref[cells] = goal
    for j in range(planes):
        reach = starts_ref[min(j, cells - 1) + 1] - starts_ref[max(j - 2, 0)]
        tiles_ref[j] = lax.shift_right_logical(reach + CAP - 1, 8)

    for j in range(planes):
        for tile in range(min(j, cells - 1) + 1 - max(j - 2, 0)):
            at = starts_ref[max(j - 2, 0)] + CAP * tile
            at = jnp.minimum(at, starts_ref[cells])
            low = jnp.bitwise_and(at, LANES - 1)
            back = jnp.bitwise_and(LANES - low, LANES - 1)
            place = pl.multiple_of(lax.shift_right_logical(at, 7) * 16, 16)
            part = [pltpu.roll(aim[pl.ds(place + 16 * n, 8), :], back, 1) for n in range(3)]
            keep = lane[0:8] < LANES - low
            spot = jnp.concatenate(
                [jnp.where(keep, part[0], part[1]), jnp.where(keep, part[1], part[2])], axis=1
            )
            x = [spot[0:1] - float(j), spot[1:2], spot[2:3]]
            size = x[0] * x[0] + x[1] * x[1] + x[2] * x[2]
            size = jnp.where(jnp.abs(spot[3:4] - float(j)) < 1.5, size, 1e30)
            slot = j * TILES + tile
            for n in range(3):
                spots[slot, n: n + 1, :] = x[n]
                part = [v.astype(jnp.float32) for v in halves(-2.0 * x[n], 3)]
                for r, p in enumerate((0, 1, 0, 1, 2, 0)):
                    line[slot, 6 * n + r: 6 * n + r + 1, :] = part[p]
            line[slot, 18:21, :] = jnp.ones((3, CAP), jnp.float32)
            for r, p in enumerate(halves(size, 3)):
                line[slot, 21 + r: 22 + r, :] = p.astype(jnp.float32)
            right_d[slot] = line[slot].astype(jnp.bfloat16)

    def describe(j, g):
        start = (j * BLOCKS + g * 8) * 16
        row = jnp.swapaxes(jnp.stack([raw[start + 16 * q: start + 16 * q + 8, :] for q in range(8)]), 0, 1)
        row = [row[r] for r in range(8)] + [raw[pl.ds(start + 8, 8, stride=16), :]]
        rows3, rows5 = features(row[0:3], row[3:6], row[6:9])
        base = (j * BLOCKS + g * 8) * NUM
        def spread(ref, first, step, rows):
            for k in range(0, len(rows), 8):
                part = jnp.swapaxes(jnp.stack(rows[k: k + 8]), 0, 1)
                for q in range(8):
                    ref[first + q * step + k: first + q * step + k + 8, :] = part[q]

        none = jnp.zeros((8, LANES), jnp.float32)
        spread(feat, base, NUM, [rows3.get(r, none) for r in range(NUM3)] + [rows5.get(r, none) for r in range(NUM5)])
        y = row[0:3]
        size = y[0] * y[0] + y[1] * y[1] + (y[2] * y[2] + CORE_SQUARE)
        line_rows = []
        for n in range(3):
            part = [v.astype(jnp.float32) for v in halves(y[n], 3)]
            line_rows += [part[p] for p in (0, 0, 1, 1, 0, 2)]
        line_rows += [p.astype(jnp.float32) for p in halves(size, 3)]
        line_rows += [none + 1.0] * 3 + [none] * 8
        spread(cols, (j * BLOCKS + g * 8) * 32, 32, line_rows)

    for j in range(planes):
        describe(j, 0)
    for g in range(1, BLOCKS // 8):
        for j in range(planes):
            pl.when(steps_ref[j] > 4 * g)(functools.partial(describe, j, g))

    def rest(value):
        return value - value.astype(jnp.bfloat16).astype(jnp.float32)

    def split_body(n, state):
        j, c = state
        for part in range(2):
            index = j * CHUNKS + c + part
            for h in range(2):
                block = j * BLOCKS + 2 * (c + part) + h
                span = slice(h * LANES, (h + 1) * LANES)
                at = pl.multiple_of(block * NUM, 8)
                value = feat[pl.ds(at, NUM3), :]
                left3[index, :, span] = jnp.concatenate([value, rest(value)], axis=0).astype(
                    jnp.bfloat16
                )
                value = feat[pl.ds(at + NUM3, NUM5), :]
                second = rest(value)
                third = rest(second)
                left5[index, :, span] = jnp.concatenate(
                    [value, second, third, jnp.zeros((8, LANES), jnp.float32)], axis=0
                ).astype(jnp.bfloat16)
                turned = cols[pl.ds(pl.multiple_of(block * 32, 32), 32), :].astype(jnp.bfloat16)
                left_d[index, span, :] = jnp.transpose(turned)
        wrap = c + 2 >= steps_ref[j]
        return (
            jnp.where(wrap, jnp.minimum(j + 1, planes - 1), j),
            jnp.where(wrap, 0, c + 2),
        )

    pieces = jnp.int32(0)
    for j in range(planes):
        pieces = pieces + lax.shift_right_logical(steps_ref[j] + 1, 1)
    lax.fori_loop(0, pieces, split_body, (jnp.int32(0), jnp.int32(0)))

    def advance(item):
        j, tile, c = item
        wrap = c + 1 >= steps_ref[j]
        turn = wrap & (tile + 1 >= tiles_ref[j])
        end = turn & (j + 1 >= planes)
        new_j = jnp.where(turn, jnp.minimum(j + 1, planes - 1), j)
        new_tile = jnp.where(turn, 0, jnp.where(wrap, tile + 1, tile))
        new_c = jnp.where(wrap, 0, c + 1)
        return (new_j, jnp.where(end, tile, new_tile), jnp.where(end, c, new_c))

    def weigh(item, buf):
        j, tile, c = item
        apart = mm(left_d[j * CHUNKS + c], right_d[j * TILES + tile])
        for s in range(CAP // 16):
            span = slice(s * 16, (s + 1) * 16)
            inv = lax.rsqrt(apart[span, :])
            square = inv * inv
            cube = square * inv
            fifth = cube * square
            buf[0, span, :], buf[1, span, :] = halves(cube, 2)
            buf[2, span, :], buf[3, span, :] = halves(fifth, 2)

    def gather(item, buf, live):
        j, tile, c = item
        index = j * CHUNKS + c
        slot = jnp.where(live, j * TILES + tile, planes * TILES)
        a = mm(left3[index], buf[0])
        b = mm(left3[index, 0:32, :], buf[1])
        d = mm(left5[index], buf[2])
        e = mm(left5[index, 0:2 * NUM5, :], buf[3])
        old = jnp.where(c == 0, 0.0, acc[slot])
        acc[slot, 0:NUM3, :] = old[0:NUM3] + (a[0:NUM3] + (a[NUM3:] + b[0:NUM3]))
        acc[slot, NUM3:, :] = old[NUM3:] + (
            d[0:NUM5] + (d[NUM5:2 * NUM5] + e[0:NUM5]) + (d[2 * NUM5:3 * NUM5] + e[NUM5:])
        )

    count = jnp.int32(0)
    for j in range(planes):
        count = count + steps_ref[j] * tiles_ref[j]

    def work(m, item):
        after = advance(item)
        weigh(after, buf_b)
        gather(item, buf_a, True)
        later = advance(after)
        weigh(later, buf_a)
        gather(after, buf_b, 2 * m + 1 < count)
        return later

    first = (jnp.int32(0), jnp.int32(0), jnp.int32(0))
    weigh(first, buf_a)
    lax.fori_loop(0, lax.shift_right_logical(count + 1, 1), work, first)

    def finish(j, tile):
        slot = j * TILES + tile
        x = [spots[slot, n: n + 1, :] for n in range(3)]
        both = acc[slot, 0:NUM3, :] + acc[slot, NUM3:2 * NUM3, :]
        linear = both[18:24] + x[0] * both[0:6] + x[1] * both[6:12] + x[2] * both[12:18]
        second = acc[slot, 2 * NUM3:, :]
        v = [
            x[0] * second[n: n + 1] + x[1] * second[3 + n: 4 + n] + x[2] * second[6 + n: 7 + n]
            for n in range(3)
        ]
        scale = 0.5 * (
            second[0:1] + second[4:5] + second[8:9]
            + x[0] * second[9:10] + x[1] * second[10:11] + x[2] * second[11:12]
        )
        v = [v[n] + scale * x[n] for n in range(3)]
        bend = jnp.concatenate([x[a] * v[b] + x[b] * v[a] for a, b in PAIRS], axis=0)
        value = linear + bend
        value = jnp.concatenate([value, jnp.zeros((2, CAP), jnp.float32)], axis=0)
        at = starts_ref[max(j - 2, 0)] + CAP * tile
        low = jnp.bitwise_and(at, LANES - 1)
        place = pl.multiple_of(lax.shift_right_logical(at, 7) * 8, 8)
        keep = lane[0:8] >= low
        one = pltpu.roll(value[:, 0:LANES], low, 1)
        two = pltpu.roll(value[:, LANES:], low, 1)
        total[pl.ds(place, 8), :] += jnp.where(keep, one, 0.0)
        total[pl.ds(place + 8, 8), :] += jnp.where(keep, two, one)
        total[pl.ds(place + 16, 8), :] += jnp.where(keep, 0.0, two)

    for j in range(planes):
        finish(j, 0)
    for j in range(planes):
        for tile in range(1, min(j, cells - 1) + 1 - max(j - 2, 0)):
            pl.when(tile < tiles_ref[j])(functools.partial(finish, j, tile))

    for i in range(cells):
        at = starts_ref[i]
        low = jnp.bitwise_and(at, LANES - 1)
        back = jnp.bitwise_and(LANES - low, LANES - 1)
        place = pl.multiple_of(lax.shift_right_logical(at, 7) * 8, 8)
        part = [pltpu.roll(total[pl.ds(place + 8 * n, 8), :], back, 1) for n in range(3)]
        keep = lane[0:8] < LANES - low
        out_ref[i, :, 0:LANES] = jnp.where(keep, part[0], part[1])
        out_ref[i, :, LANES:] = jnp.where(keep, part[1], part[2])


def near_call(before, sheet, after):
    planes = sheet.shape[0] // (3 * ROWS)
    cells = planes - 2
    vmem = pl.BlockSpec(memory_space=pltpu.VMEM)
    return pl.pallas_call(
        functools.partial(near_kernel, planes),
        out_shape=jax.ShapeDtypeStruct((cells, 8, CAP), jnp.float32),
        in_specs=[vmem, vmem, vmem],
        out_specs=vmem,
        scratch_shapes=[
            pltpu.VMEM((planes * BLOCKS * 16, LANES), jnp.float32),
            pltpu.VMEM((planes * BLOCKS * NUM, LANES), jnp.float32),
            pltpu.VMEM((planes * BLOCKS * 32, LANES), jnp.float32),
            pltpu.VMEM((planes * CHUNKS, 48, CAP), jnp.bfloat16),
            pltpu.VMEM((planes * CHUNKS, 128, CAP), jnp.bfloat16),
            pltpu.VMEM((planes * CHUNKS, CAP, 32), jnp.bfloat16),
            pltpu.VMEM((planes * TILES, 32, CAP), jnp.bfloat16),
            pltpu.VMEM((planes * TILES, 8, CAP), jnp.float32),
            pltpu.VMEM((planes * TILES, 32, CAP), jnp.float32),
            pltpu.VMEM((4, CAP, CAP), jnp.bfloat16),
            pltpu.VMEM((4, CAP, CAP), jnp.bfloat16),
            pltpu.VMEM((planes * TILES + 1, NUM, CAP), jnp.float32),
            pltpu.VMEM((10 * 16, LANES), jnp.float32),
            pltpu.VMEM((10 * 8, LANES), jnp.float32),
            pltpu.SMEM((planes,), jnp.int32),
            pltpu.SMEM((cells + 1,), jnp.int32),
            pltpu.SMEM((planes,), jnp.int32),
        ],
        compiler_params=pltpu.CompilerParams(vmem_limit_bytes=40 * 1024 * 1024),
        cost_estimate=pl.CostEstimate(flops=3 * 10**10, bytes_accessed=10**7, transcendentals=0),
        name="near",
    )(before, sheet, after)


def far_kernel(planes, spans, moment_ref, applied_ref, sheet_ref, total, out_ref):
    cells = planes - 2
    span_x, span_y, span_z = spans
    shape = (span_z, LANES)
    half = LANES // 2
    column = lax.broadcasted_iota(jnp.int32, shape, 1)
    moment = []
    for m in range(9):
        value = moment_ref[:, 0, m // 2 * LANES: (m // 2 + 1) * LANES]
        if m % 2:
            value = pltpu.roll(value, half, 1)
        moment.append(jnp.where(column < half, value, 0.0))
    device = column // cells
    source = (
        (device // span_y * cells + column % cells).astype(jnp.float32),
        (device % span_y).astype(jnp.float32),
        lax.broadcasted_iota(jnp.int32, shape, 0).astype(jnp.float32),
    )
    w = (moment[5] - moment[7], moment[6] - moment[2], moment[1] - moment[3])
    index = {}
    for n, (a, b) in enumerate(PAIRS):
        index[a, b] = index[b, a] = n
    pieces = []
    for i in range(cells):
        mine = (lax.axis_index("gx") * cells + i, lax.axis_index("gy"), lax.axis_index("gz"))
        r = [mine[n].astype(jnp.float32) - source[n] for n in range(3)]
        reach = jnp.maximum(jnp.maximum(jnp.abs(r[0]), jnp.abs(r[1])), jnp.abs(r[2]))
        inv = lax.rsqrt(r[0] * r[0] + r[1] * r[1] + r[2] * r[2] + CORE_SQUARE)
        inv = jnp.where(reach > 1.5, inv, 0.0)
        cube = inv * inv * inv
        fifth = cube * inv * inv
        radial = 2.0 * cube + KAPPA * fifth
        along = w[0] * r[0] + w[1] * r[1] + w[2] * r[2]
        turn = [cross(r, (moment[n], moment[3 + n], moment[6 + n])) for n in range(3)]
        slope = (3.0 * SECOND) * along * fifth
        cut = SECOND * cube
        bulk = SECOND * along * (radial - cube)
        front = -FIRST * radial
        for n, (a, b) in enumerate(PAIRS):
            element = (
                front * (turn[b][a] + turn[a][b])
                + slope * r[a] * r[b]
                - cut * (w[a] * r[b] + w[b] * r[a])
            )
            if a == b:
                element = element + bulk
            pieces.append(plus([element[k: k + 8] for k in range(0, span_z, 8)]))
    pieces = [
        jnp.sum(jnp.sum(jnp.swapaxes(jnp.stack(pieces[k: k + 8]), 0, 1), axis=0), axis=1, keepdims=True)
        for k in range(0, len(pieces), 8)
    ]
    for i in range(cells):
        stress = []
        for n, (a, b) in enumerate(PAIRS):
            k = 6 * i + n
            stress.append(
                pieces[k // 8][k % 8: k % 8 + 1]
                + 0.5 * (applied_ref[a: a + 1, b: b + 1] + applied_ref[b: b + 1, a: a + 1])
                + total[i, n: n + 1, :]
            )
        row = ROWS * (planes + 1 + i)
        t = [sheet_ref[row + 3 + n: row + 4 + n, :] for n in range(3)]
        b = [sheet_ref[row + 6 + n: row + 7 + n, :] for n in range(3)]
        force = [plus([stress[index[m, n]] * b[n] for n in range(3)]) for m in range(3)]
        for n, value in enumerate(cross(force, t)):
            out_ref[n, i, 0, :, :] = value


def pack_kernel(counts_ref, offset_ref, vector_ref, burgers_ref, all_ref, hold, count_hold, sems):
    cells = offset_ref.shape[1]
    copies = [
        pltpu.make_async_copy(ref, hold.at[n], sems.at[n])
        for n, ref in enumerate((offset_ref, vector_ref, burgers_ref))
    ]
    number = pltpu.make_async_copy(counts_ref, count_hold, sems.at[3])
    number.start()
    for copy in copies:
        copy.start()
    number.wait()
    slot = lax.broadcasted_iota(jnp.int32, (cells, CAP), 1)
    cell = lax.broadcasted_iota(jnp.int32, (cells, CAP), 0)
    live = jnp.zeros((cells, CAP), jnp.int32)
    for i in range(cells):
        live = jnp.where(cell == i, count_hold[i], live)
    filled = slot < live
    for copy in copies:
        copy.wait()
    flat = [hold[n].reshape(3, cells, CAP) for n in range(3)]
    offset = [flat[0][n] for n in range(3)]
    tangent = [jnp.where(filled, flat[1][n], 0.0) for n in range(3)]
    charge = [jnp.where(filled, flat[2][n], 0.0) for n in range(3)]
    level = live.astype(jnp.float32)
    for m in range(3):
        for k in range(3):
            value = jnp.sum(charge[m] * tangent[k], axis=1, keepdims=True)
            level = jnp.where(slot == LANES + 3 * m + k, value, level)
    rows = offset + tangent + charge + [level]
    packed = jnp.concatenate([v[i: i + 1] for i in range(cells) for v in rows], axis=0)
    for d in range(all_ref.shape[0]):
        all_ref[d] = packed


def pick_kernel(planes, spans, all_ref, sheet_ref, moment_ref):
    span_x, span_y, span_z = spans
    cells = planes - 2
    for dy in range(3):
        y = lax.axis_index("gy") + (dy - 1)
        for j in range(planes):
            step = (j + cells - 1) // cells - 1
            c = (j - 1) % cells
            x = lax.axis_index("gx") + step
            inside = (x >= 0) & (x < span_x) & (y >= 0) & (y < span_y)
            device = jnp.clip(x, 0, span_x - 1) * span_y + jnp.clip(y, 0, span_y - 1)
            row = ROWS * (dy * planes + j)
            sheet_ref[row: row + ROWS, :] = jnp.where(
                inside, all_ref[device, ROWS * c: ROWS * c + ROWS, :], 0.0
            )
    rows = [
        all_ref[d, ROWS * c + ROWS - 1: ROWS * c + ROWS, LANES:]
        for d in range(span_x * span_y)
        for c in range(cells)
    ]
    rows.append(jnp.zeros((LANES - len(rows), LANES), jnp.float32))
    flip = jnp.transpose(jnp.concatenate(rows, axis=0))
    half = LANES // 2
    line = [
        flip[2 * r: 2 * r + 1] + pltpu.roll(flip[2 * r + 1: 2 * r + 2], half, 1) for r in range(5)
    ]
    line = jnp.concatenate(line, axis=1)
    moment_ref[...] = jnp.broadcast_to(line[None], moment_ref.shape)


def beside(first, last, axis):
    devices = lax.axis_size(axis)
    up = [(i, (i + 1) % devices) for i in range(devices)]
    down = [(i + 1, i) for i in range(devices - 1)]
    return lax.ppermute(last, axis, up), lax.ppermute(first, axis, down)


def local(seg_offset, seg_vector, burgers, cell_counts, applied):
    cells = seg_offset.shape[1]
    planes = cells + 2
    spans = tuple(lax.axis_size(a) for a in ("gx", "gy", "gz"))
    devices = spans[0] * spans[1]
    vmem = pl.BlockSpec(memory_space=pltpu.VMEM)
    anywhere = pl.BlockSpec(memory_space=pl.ANY)
    limit = pltpu.CompilerParams(vmem_limit_bytes=40 * 1024 * 1024)
    packed = pl.pallas_call(
        pack_kernel,
        out_shape=jax.ShapeDtypeStruct((devices, cells * ROWS, CAP), jnp.float32),
        in_specs=[anywhere] * 4,
        out_specs=vmem,
        scratch_shapes=[
            pltpu.VMEM((3,) + seg_offset.shape, jnp.float32),
            pltpu.SMEM((cells,), jnp.int32),
            pltpu.SemaphoreType.DMA((4,)),
        ],
        compiler_params=pltpu.CompilerParams(vmem_limit_bytes=60 * 1024 * 1024),
        name="pack",
    )(cell_counts.reshape(cells), seg_offset, seg_vector, burgers)
    every = lax.all_to_all(packed, ("gx", "gy"), 0, 0)
    sheet, moments = pl.pallas_call(
        functools.partial(pick_kernel, planes, spans),
        out_shape=(
            jax.ShapeDtypeStruct((3 * planes * ROWS, CAP), jnp.float32),
            jax.ShapeDtypeStruct((spans[2], 1, 5 * LANES), jnp.float32),
        ),
        in_specs=[vmem],
        out_specs=(vmem, vmem),
        compiler_params=limit,
        name="pick",
    )(every)
    before, after = beside(sheet, sheet, "gz")
    moments = lax.all_to_all(moments, "gz", 0, 0)
    total = near_call(before, sheet, after)
    return pl.pallas_call(
        functools.partial(far_kernel, planes, spans),
        out_shape=jax.ShapeDtypeStruct(seg_offset.shape, jnp.float32),
        in_specs=[vmem] * 4,
        out_specs=vmem,
        compiler_params=limit,
        name="far",
    )(moments, applied, sheet, total)


def solution(mesh):
    placed = P(None, "gx", "gy", "gz", None)
    return jax.shard_map(
        local,
        mesh=mesh,
        in_specs=(placed, placed, placed, P("gx", "gy", "gz"), P()),
        out_specs=placed,
        check_vma=False,
    )
```

```python
import functools
import math

import jax
import jax.numpy as jnp
from jax import lax
from jax.experimental import pallas as pl
from jax.experimental.pallas import tpu as pltpu
from jax.sharding import PartitionSpec as P

CORE_SQUARE = 0.2 * 0.2
FIRST = 1.0 / (8.0 * math.pi)
SECOND = 1.0 / (4.0 * math.pi * 0.7)
KAPPA = 3.0 * CORE_SQUARE
CAP = 256
LANES = 128
ROWS = 10
PAIRS = ((0, 0), (0, 1), (0, 2), (1, 1), (1, 2), (2, 2))
NUM3 = 24
NUM5 = 40
NUM = NUM3 + NUM5
BLOCKS = 24
CHUNKS = 10
TILES = 3


def cross(a, b):
    return (
        a[1] * b[2] - a[2] * b[1],
        a[2] * b[0] - a[0] * b[2],
        a[0] * b[1] - a[1] * b[0],
    )


def plus(terms):
    terms = [t for t in terms if t is not None]
    total = terms[0]
    for t in terms[1:]:
        total = total + t
    return total


def features(y, t, b):
    w = cross(b, t)
    turn = [[None, b[2], -b[1]], [-b[2], None, b[0]], [b[1], -b[0], None]]
    c2w = [SECOND * v for v in w]
    lin3, lin5 = {}, {}
    for n, (i, j) in enumerate(PAIRS):
        for m in range(3):
            parts = []
            if turn[i][m] is not None:
                parts.append(turn[i][m] * t[j])
            if turn[j][m] is not None:
                parts.append(turn[j][m] * t[i])
            base = plus(parts) * (-FIRST) if parts else None
            a3 = [2.0 * base] if base is not None else []
            a5 = [base] if base is not None else []
            if i == j:
                a3.append(c2w[m])
                a5.append(c2w[m])
            if m == j:
                a3.append(-c2w[i])
            if m == i:
                a3.append(-c2w[j])
            lin3[m, n] = plus(a3) if a3 else None
            lin5[m, n] = KAPPA * plus(a5) if a5 else None
    w3 = [3.0 * v for v in c2w]
    wy = [[w3[m] * y[n] for n in range(3)] for m in range(3)]
    dot = wy[0][0] + wy[1][1] + wy[2][2]
    doty = [dot * y[n] for n in range(3)]
    rows3, rows5 = {}, {}
    for n, (i, j) in enumerate(PAIRS):
        zero3, zero5 = [], [doty[i] * y[j]]
        for m in range(3):
            if lin3[m, n] is not None:
                rows3[6 * m + n] = lin3[m, n]
                zero3.append(lin3[m, n] * y[m])
            quad = [wy[m][i] * y[j]]
            if m == i:
                quad.append(doty[j])
            if m == j:
                quad.append(doty[i])
            if lin5[m, n] is not None:
                quad.append(lin5[m, n])
                zero5.append(lin5[m, n] * y[m])
            rows5[6 * m + n] = plus(quad)
        if zero3:
            rows3[18 + n] = -plus(zero3)
        rows5[18 + n] = -plus(zero5)
    for m in range(3):
        for n in range(3):
            rows5[24 + 3 * m + n] = -wy[m][n]
        rows5[33 + m] = w3[m]
    return rows3, rows5


def halves(value, terms):
    out = []
    for k in range(terms):
        part = value.astype(jnp.bfloat16)
        out.append(part)
        if k + 1 < terms:
            value = value - part.astype(jnp.float32)
    return out


def near_kernel(
    planes, before_ref, middle_ref, after_ref, out_ref,
    raw, feat, cols, left3, left5, left_d, right_d, spots, line, buf_a, buf_b, acc, aim, total, steps_ref, starts_ref, tiles_ref,
):
    sources = (before_ref, middle_ref, after_ref)
    cells = planes - 2
    columns = [(k, c) for k in (0, 2, 1) for c in range(3)]
    lane = lax.broadcasted_iota(jnp.int32, (16, LANES), 1)
    lift = lax.broadcasted_iota(jnp.int32, (16, LANES), 0)
    mm = functools.partial(jnp.dot, preferred_element_type=jnp.float32)
    for ref in (raw, aim, total, line):
        ref[...] = jnp.zeros_like(ref)

    def append(ref, first, second, at, offset):
        rows = first.shape[0]
        low = jnp.bitwise_and(at, LANES - 1)
        base = lax.shift_right_logical(at, 7) + offset
        first = pltpu.roll(first, low, 1)
        second = pltpu.roll(second, low, 1)
        keep = lane[0:rows] >= low
        place = pl.multiple_of(base * 16, 16)
        ref[pl.ds(place, rows), :] = jnp.where(keep, first, ref[pl.ds(place, rows), :])
        ref[pl.ds(place + 16, rows), :] = jnp.where(keep, second, first)
        ref[pl.ds(place + 32, rows), :] = jnp.where(keep, 0.0, second)

    goal = jnp.int32(0)
    for j in range(planes):
        at = jnp.int32(0)
        for k, c in columns:
            row = ROWS * (c * planes + j)
            first = sources[k][row: row + ROWS, 0:LANES]
            second = sources[k][row: row + ROWS, LANES:]
            count = first[ROWS - 1: ROWS, 0:1].astype(jnp.int32)[0, 0]
            if k != 1:
                edge = 0 if k == 0 else lax.axis_size("gz") - 1
                count = jnp.where(lax.axis_index("gz") == edge, 0, count)
            if k == 1 and c == 1 and 0 < j < planes - 1:
                shift = jnp.where(lift[0:8] == 0, j - 0.5, -0.5)
                mark = lift[0:8] < 3
                starts_ref[j - 1] = goal
                append(
                    aim,
                    jnp.where(mark, first[0:8] + shift, float(j)),
                    jnp.where(mark, second[0:8] + shift, float(j)),
                    goal,
                    0,
                )
                goal = goal + count
            shift = (
                jnp.where(lift < 3, -0.5, 0.0)
                + jnp.where(lift == 1, float(c - 1), 0.0)
                + jnp.where(lift == 2, float(k - 1), 0.0)
            )[0:ROWS]
            append(raw, first + shift, second + shift, at, j * BLOCKS)
            at = at + count
        steps_ref[j] = jnp.maximum(lax.shift_right_logical(at + CAP - 1, 8), 1)
    starts_ref[cells] = goal
    for j in range(planes):
        reach = starts_ref[min(j, cells - 1) + 1] - starts_ref[max(j - 2, 0)]
        tiles_ref[j] = lax.shift_right_logical(reach + CAP - 1, 8)

    for j in range(planes):
        for tile in range(min(j, cells - 1) + 1 - max(j - 2, 0)):
            at = starts_ref[max(j - 2, 0)] + CAP * tile
            at = jnp.minimum(at, starts_ref[cells])
            low = jnp.bitwise_and(at, LANES - 1)
            back = jnp.bitwise_and(LANES - low, LANES - 1)
            place = pl.multiple_of(lax.shift_right_logical(at, 7) * 16, 16)
            part = [pltpu.roll(aim[pl.ds(place + 16 * n, 8), :], back, 1) for n in range(3)]
            keep = lane[0:8] < LANES - low
            spot = jnp.concatenate(
                [jnp.where(keep, part[0], part[1]), jnp.where(keep, part[1], part[2])], axis=1
            )
            x = [spot[0:1] - float(j), spot[1:2], spot[2:3]]
            size = x[0] * x[0] + x[1] * x[1] + x[2] * x[2]
            size = jnp.where(jnp.abs(spot[3:4] - float(j)) < 1.5, size, 1e30)
            slot = j * TILES + tile
            for n in range(3):
                spots[slot, n: n + 1, :] = x[n]
                part = [v.astype(jnp.float32) for v in halves(-2.0 * x[n], 3)]
                for r, p in enumerate((0, 1, 0, 1, 2, 0)):
                    line[slot, 6 * n + r: 6 * n + r + 1, :] = part[p]
            line[slot, 18:21, :] = jnp.ones((3, CAP), jnp.float32)
            for r, p in enumerate(halves(size, 3)):
                line[slot, 21 + r: 22 + r, :] = p.astype(jnp.float32)
            right_d[slot] = line[slot].astype(jnp.bfloat16)

    def describe(j, g):
        start = (j * BLOCKS + g * 8) * 16
        row = jnp.swapaxes(jnp.stack([raw[start + 16 * q: start + 16 * q + 8, :] for q in range(8)]), 0, 1)
        row = [row[r] for r in range(8)] + [raw[pl.ds(start + 8, 8, stride=16), :]]
        rows3, rows5 = features(row[0:3], row[3:6], row[6:9])
        base = (j * BLOCKS + g * 8) * NUM
        def spread(ref, first, step, rows):
            for k in range(0, len(rows), 8):
                part = jnp.swapaxes(jnp.stack(rows[k: k + 8]), 0, 1)
                for q in range(8):
                    ref[first + q * step + k: first + q * step + k + 8, :] = part[q]

        none = jnp.zeros((8, LANES), jnp.float32)
        spread(feat, base, NUM, [rows3.get(r, none) for r in range(NUM3)] + [rows5.get(r, none) for r in range(NUM5)])
        y = row[0:3]
        size = y[0] * y[0] + y[1] * y[1] + (y[2] * y[2] + CORE_SQUARE)
        line_rows = []
        for n in range(3):
            part = [v.astype(jnp.float32) for v in halves(y[n], 3)]
            line_rows += [part[p] for p in (0, 0, 1, 1, 0, 2)]
        line_rows += [p.astype(jnp.float32) for p in halves(size, 3)]
        line_rows += [none + 1.0] * 3 + [none] * 8
        spread(cols, (j * BLOCKS + g * 8) * 32, 32, line_rows)

    for j in range(planes):
        describe(j, 0)
    for g in range(1, BLOCKS // 8):
        for j in range(planes):
            pl.when(steps_ref[j] > 4 * g)(functools.partial(describe, j, g))

    def rest(value):
        return value - value.astype(jnp.bfloat16).astype(jnp.float32)

    def split_body(n, state):
        j, c = state
        for part in range(2):
            index = j * CHUNKS + c + part
            for h in range(2):
                block = j * BLOCKS + 2 * (c + part) + h
                span = slice(h * LANES, (h + 1) * LANES)
                at = pl.multiple_of(block * NUM, 8)
                value = feat[pl.ds(at, NUM3), :]
                left3[index, :, span] = jnp.concatenate([value, rest(value)], axis=0).astype(
                    jnp.bfloat16
                )
                value = feat[pl.ds(at + NUM3, NUM5), :]
                second = rest(value)
                third = rest(second)
                left5[index, :, span] = jnp.concatenate(
                    [value, second, third, jnp.zeros((8, LANES), jnp.float32)], axis=0
                ).astype(jnp.bfloat16)
                turned = cols[pl.ds(pl.multiple_of(block * 32, 32), 32), :].astype(jnp.bfloat16)
                left_d[index, span, :] = jnp.transpose(turned)
        wrap = c + 2 >= steps_ref[j]
        return (
            jnp.where(wrap, jnp.minimum(j + 1, planes - 1), j),
            jnp.where(wrap, 0, c + 2),
        )

    pieces = jnp.int32(0)
    for j in range(planes):
        pieces = pieces + lax.shift_right_logical(steps_ref[j] + 1, 1)
    lax.fori_loop(0, pieces, split_body, (jnp.int32(0), jnp.int32(0)))

    def advance(item):
        j, tile, c = item
        wrap = c + 1 >= steps_ref[j]
        turn = wrap & (tile + 1 >= tiles_ref[j])
        end = turn & (j + 1 >= planes)
        new_j = jnp.where(turn, jnp.minimum(j + 1, planes - 1), j)
        new_tile = jnp.where(turn, 0, jnp.where(wrap, tile + 1, tile))
        new_c = jnp.where(wrap, 0, c + 1)
        return (new_j, jnp.where(end, tile, new_tile), jnp.where(end, c, new_c))

    def weigh(item, buf):
        j, tile, c = item
        apart = mm(left_d[j * CHUNKS + c], right_d[j * TILES + tile])
        for s in range(CAP // 16):
            span = slice(s * 16, (s + 1) * 16)
            inv = lax.rsqrt(apart[span, :])
            square = inv * inv
            cube = square * inv
            fifth = cube * square
            buf[0, span, :], buf[1, span, :] = halves(cube, 2)
            buf[2, span, :], buf[3, span, :] = halves(fifth, 2)

    def gather(item, buf, live):
        j, tile, c = item
        index = j * CHUNKS + c
        slot = jnp.where(live, j * TILES + tile, planes * TILES)
        a = mm(left3[index], buf[0])
        b = mm(left3[index, 0:32, :], buf[1])
        d = mm(left5[index], buf[2])
        e = mm(left5[index, 0:2 * NUM5, :], buf[3])
        old = jnp.where(c == 0, 0.0, acc[slot])
        acc[slot, 0:NUM3, :] = old[0:NUM3] + (a[0:NUM3] + (a[NUM3:] + b[0:NUM3]))
        acc[slot, NUM3:, :] = old[NUM3:] + (
            d[0:NUM5] + (d[NUM5:2 * NUM5] + e[0:NUM5]) + (d[2 * NUM5:3 * NUM5] + e[NUM5:])
        )

    count = jnp.int32(0)
    for j in range(planes):
        count = count + steps_ref[j] * tiles_ref[j]

    def work(m, item):
        after = advance(item)
        weigh(after, buf_b)
        gather(item, buf_a, True)
        later = advance(after)
        weigh(later, buf_a)
        gather(after, buf_b, 2 * m + 1 < count)
        return later

    first = (jnp.int32(0), jnp.int32(0), jnp.int32(0))
    weigh(first, buf_a)
    lax.fori_loop(0, lax.shift_right_logical(count + 1, 1), work, first)

    def finish(j, tile):
        slot = j * TILES + tile
        x = [spots[slot, n: n + 1, :] for n in range(3)]
        both = acc[slot, 0:NUM3, :] + acc[slot, NUM3:2 * NUM3, :]
        linear = both[18:24] + x[0] * both[0:6] + x[1] * both[6:12] + x[2] * both[12:18]
        second = acc[slot, 2 * NUM3:, :]
        v = [
            x[0] * second[n: n + 1] + x[1] * second[3 + n: 4 + n] + x[2] * second[6 + n: 7 + n]
            for n in range(3)
        ]
        scale = 0.5 * (
            second[0:1] + second[4:5] + second[8:9]
            + x[0] * second[9:10] + x[1] * second[10:11] + x[2] * second[11:12]
        )
        v = [v[n] + scale * x[n] for n in range(3)]
        bend = jnp.concatenate([x[a] * v[b] + x[b] * v[a] for a, b in PAIRS], axis=0)
        value = linear + bend
        value = jnp.concatenate([value, jnp.zeros((2, CAP), jnp.float32)], axis=0)
        at = starts_ref[max(j - 2, 0)] + CAP * tile
        low = jnp.bitwise_and(at, LANES - 1)
        place = pl.multiple_of(lax.shift_right_logical(at, 7) * 8, 8)
        keep = lane[0:8] >= low
        one = pltpu.roll(value[:, 0:LANES], low, 1)
        two = pltpu.roll(value[:, LANES:], low, 1)
        total[pl.ds(place, 8), :] += jnp.where(keep, one, 0.0)
        total[pl.ds(place + 8, 8), :] += jnp.where(keep, two, one)
        total[pl.ds(place + 16, 8), :] += jnp.where(keep, 0.0, two)

    for j in range(planes):
        finish(j, 0)
    for j in range(planes):
        for tile in range(1, min(j, cells - 1) + 1 - max(j - 2, 0)):
            pl.when(tile < tiles_ref[j])(functools.partial(finish, j, tile))

    for i in range(cells):
        at = starts_ref[i]
        low = jnp.bitwise_and(at, LANES - 1)
        back = jnp.bitwise_and(LANES - low, LANES - 1)
        place = pl.multiple_of(lax.shift_right_logical(at, 7) * 8, 8)
        part = [pltpu.roll(total[pl.ds(place + 8 * n, 8), :], back, 1) for n in range(3)]
        keep = lane[0:8] < LANES - low
        out_ref[i, :, 0:LANES] = jnp.where(keep, part[0], part[1])
        out_ref[i, :, LANES:] = jnp.where(keep, part[1], part[2])


def near_call(before, sheet, after):
    planes = sheet.shape[0] // (3 * ROWS)
    cells = planes - 2
    vmem = pl.BlockSpec(memory_space=pltpu.VMEM)
    return pl.pallas_call(
        functools.partial(near_kernel, planes),
        out_shape=jax.ShapeDtypeStruct((cells, 8, CAP), jnp.float32),
        in_specs=[vmem, vmem, vmem],
        out_specs=vmem,
        scratch_shapes=[
            pltpu.VMEM((planes * BLOCKS * 16, LANES), jnp.float32),
            pltpu.VMEM((planes * BLOCKS * NUM, LANES), jnp.float32),
            pltpu.VMEM((planes * BLOCKS * 32, LANES), jnp.float32),
            pltpu.VMEM((planes * CHUNKS, 48, CAP), jnp.bfloat16),
            pltpu.VMEM((planes * CHUNKS, 128, CAP), jnp.bfloat16),
            pltpu.VMEM((planes * CHUNKS, CAP, 32), jnp.bfloat16),
            pltpu.VMEM((planes * TILES, 32, CAP), jnp.bfloat16),
            pltpu.VMEM((planes * TILES, 8, CAP), jnp.float32),
            pltpu.VMEM((planes * TILES, 32, CAP), jnp.float32),
            pltpu.VMEM((4, CAP, CAP), jnp.bfloat16),
            pltpu.VMEM((4, CAP, CAP), jnp.bfloat16),
            pltpu.VMEM((planes * TILES + 1, NUM, CAP), jnp.float32),
            pltpu.VMEM((10 * 16, LANES), jnp.float32),
            pltpu.VMEM((10 * 8, LANES), jnp.float32),
            pltpu.SMEM((planes,), jnp.int32),
            pltpu.SMEM((cells + 1,), jnp.int32),
            pltpu.SMEM((planes,), jnp.int32),
        ],
        compiler_params=pltpu.CompilerParams(vmem_limit_bytes=40 * 1024 * 1024),
        cost_estimate=pl.CostEstimate(flops=3 * 10**10, bytes_accessed=10**7, transcendentals=0),
        name="near",
    )(before, sheet, after)


def far_kernel(planes, spans, moment_ref, applied_ref, sheet_ref, total, out_ref):
    cells = planes - 2
    span_x, span_y, span_z = spans
    shape = (span_z, LANES)
    half = LANES // 2
    column = lax.broadcasted_iota(jnp.int32, shape, 1)
    moment = []
    for m in range(9):
        value = moment_ref[:, 0, m // 2 * LANES: (m // 2 + 1) * LANES]
        if m % 2:
            value = pltpu.roll(value, half, 1)
        moment.append(jnp.where(column < half, value, 0.0))
    device = column // cells
    source = (
        (device // span_y * cells + column % cells).astype(jnp.float32),
        (device % span_y).astype(jnp.float32),
        lax.broadcasted_iota(jnp.int32, shape, 0).astype(jnp.float32),
    )
    w = (moment[5] - moment[7], moment[6] - moment[2], moment[1] - moment[3])
    index = {}
    for n, (a, b) in enumerate(PAIRS):
        index[a, b] = index[b, a] = n
    pieces = []
    for i in range(cells):
        mine = (lax.axis_index("gx") * cells + i, lax.axis_index("gy"), lax.axis_index("gz"))
        r = [mine[n].astype(jnp.float32) - source[n] for n in range(3)]
        reach = jnp.maximum(jnp.maximum(jnp.abs(r[0]), jnp.abs(r[1])), jnp.abs(r[2]))
        inv = lax.rsqrt(r[0] * r[0] + r[1] * r[1] + r[2] * r[2] + CORE_SQUARE)
        inv = jnp.where(reach > 1.5, inv, 0.0)
        cube = inv * inv * inv
        fifth = cube * inv * inv
        radial = 2.0 * cube + KAPPA * fifth
        along = w[0] * r[0] + w[1] * r[1] + w[2] * r[2]
        turn = [cross(r, (moment[n], moment[3 + n], moment[6 + n])) for n in range(3)]
        slope = (3.0 * SECOND) * along * fifth
        cut = SECOND * cube
        bulk = SECOND * along * (radial - cube)
        front = -FIRST * radial
        for n, (a, b) in enumerate(PAIRS):
            element = (
                front * (turn[b][a] + turn[a][b])
                + slope * r[a] * r[b]
                - cut * (w[a] * r[b] + w[b] * r[a])
            )
            if a == b:
                element = element + bulk
            pieces.append(plus([element[k: k + 8] for k in range(0, span_z, 8)]))
    pieces = [
        jnp.sum(jnp.sum(jnp.swapaxes(jnp.stack(pieces[k: k + 8]), 0, 1), axis=0), axis=1, keepdims=True)
        for k in range(0, len(pieces), 8)
    ]
    for i in range(cells):
        stress = []
        for n, (a, b) in enumerate(PAIRS):
            k = 6 * i + n
            stress.append(
                pieces[k // 8][k % 8: k % 8 + 1]
                + 0.5 * (applied_ref[a: a + 1, b: b + 1] + applied_ref[b: b + 1, a: a + 1])
                + total[i, n: n + 1, :]
            )
        row = ROWS * (planes + 1 + i)
        t = [sheet_ref[row + 3 + n: row + 4 + n, :] for n in range(3)]
        b = [sheet_ref[row + 6 + n: row + 7 + n, :] for n in range(3)]
        force = [plus([stress[index[m, n]] * b[n] for n in range(3)]) for m in range(3)]
        for n, value in enumerate(cross(force, t)):
            out_ref[n, i, 0, :, :] = value


def pack_kernel(counts_ref, offset_ref, vector_ref, burgers_ref, all_ref, hold, count_hold, sems):
    cells = offset_ref.shape[1]
    copies = [
        pltpu.make_async_copy(ref, hold.at[n], sems.at[n])
        for n, ref in enumerate((offset_ref, vector_ref, burgers_ref))
    ]
    number = pltpu.make_async_copy(counts_ref, count_hold, sems.at[3])
    number.start()
    for copy in copies:
        copy.start()
    number.wait()
    slot = lax.broadcasted_iota(jnp.int32, (cells, CAP), 1)
    cell = lax.broadcasted_iota(jnp.int32, (cells, CAP), 0)
    live = jnp.zeros((cells, CAP), jnp.int32)
    for i in range(cells):
        live = jnp.where(cell == i, count_hold[i], live)
    filled = slot < live
    for copy in copies:
        copy.wait()
    flat = [hold[n].reshape(3, cells, CAP) for n in range(3)]
    offset = [flat[0][n] for n in range(3)]
    tangent = [jnp.where(filled, flat[1][n], 0.0) for n in range(3)]
    charge = [jnp.where(filled, flat[2][n], 0.0) for n in range(3)]
    level = live.astype(jnp.float32)
    for m in range(3):
        for k in range(3):
            value = jnp.sum(charge[m] * tangent[k], axis=1, keepdims=True)
            level = jnp.where(slot == LANES + 3 * m + k, value, level)
    rows = offset + tangent + charge + [level]
    packed = jnp.concatenate([v[i: i + 1] for i in range(cells) for v in rows], axis=0)
    for d in range(all_ref.shape[0]):
        all_ref[d] = packed


def pick_kernel(planes, spans, all_ref, sheet_ref, moment_ref):
    span_x, span_y, span_z = spans
    cells = planes - 2
    for dy in range(3):
        y = lax.axis_index("gy") + (dy - 1)
        for j in range(planes):
            step = (j + cells - 1) // cells - 1
            c = (j - 1) % cells
            x = lax.axis_index("gx") + step
            inside = (x >= 0) & (x < span_x) & (y >= 0) & (y < span_y)
            device = jnp.clip(x, 0, span_x - 1) * span_y + jnp.clip(y, 0, span_y - 1)
            row = ROWS * (dy * planes + j)
            sheet_ref[row: row + ROWS, :] = jnp.where(
                inside, all_ref[device, ROWS * c: ROWS * c + ROWS, :], 0.0
            )
    rows = [
        all_ref[d, ROWS * c + ROWS - 1: ROWS * c + ROWS, LANES:]
        for d in range(span_x * span_y)
        for c in range(cells)
    ]
    rows.append(jnp.zeros((LANES - len(rows), LANES), jnp.float32))
    flip = jnp.transpose(jnp.concatenate(rows, axis=0))
    half = LANES // 2
    line = [
        flip[2 * r: 2 * r + 1] + pltpu.roll(flip[2 * r + 1: 2 * r + 2], half, 1) for r in range(5)
    ]
    line = jnp.concatenate(line, axis=1)
    moment_ref[...] = jnp.broadcast_to(line[None], moment_ref.shape)


def beside(first, last, axis):
    devices = lax.axis_size(axis)
    up = [(i, (i + 1) % devices) for i in range(devices)]
    down = [((i + 1) % devices, i) for i in range(devices)]
    return lax.ppermute(last, axis, up), lax.ppermute(first, axis, down)


def local(seg_offset, seg_vector, burgers, cell_counts, applied):
    cells = seg_offset.shape[1]
    planes = cells + 2
    spans = tuple(lax.axis_size(a) for a in ("gx", "gy", "gz"))
    devices = spans[0] * spans[1]
    vmem = pl.BlockSpec(memory_space=pltpu.VMEM)
    anywhere = pl.BlockSpec(memory_space=pl.ANY)
    limit = pltpu.CompilerParams(vmem_limit_bytes=40 * 1024 * 1024)
    packed = pl.pallas_call(
        pack_kernel,
        out_shape=jax.ShapeDtypeStruct((devices, cells * ROWS, CAP), jnp.float32),
        in_specs=[anywhere] * 4,
        out_specs=vmem,
        scratch_shapes=[
            pltpu.VMEM((3,) + seg_offset.shape, jnp.float32),
            pltpu.SMEM((cells,), jnp.int32),
            pltpu.SemaphoreType.DMA((4,)),
        ],
        compiler_params=pltpu.CompilerParams(vmem_limit_bytes=60 * 1024 * 1024),
        name="pack",
    )(cell_counts.reshape(cells), seg_offset, seg_vector, burgers)
    every = lax.all_to_all(packed, ("gx", "gy"), 0, 0)
    sheet, moments = pl.pallas_call(
        functools.partial(pick_kernel, planes, spans),
        out_shape=(
            jax.ShapeDtypeStruct((3 * planes * ROWS, CAP), jnp.float32),
            jax.ShapeDtypeStruct((spans[2], 1, 5 * LANES), jnp.float32),
        ),
        in_specs=[vmem],
        out_specs=(vmem, vmem),
        compiler_params=limit,
        name="pick",
    )(every)
    before, after = beside(sheet, sheet, "gz")
    moments = lax.all_to_all(moments, "gz", 0, 0)
    total = near_call(before, sheet, after)
    return pl.pallas_call(
        functools.partial(far_kernel, planes, spans),
        out_shape=jax.ShapeDtypeStruct(seg_offset.shape, jnp.float32),
        in_specs=[vmem] * 4,
        out_specs=vmem,
        compiler_params=limit,
        name="far",
    )(moments, applied, sheet, total)


def solution(mesh):
    placed = P(None, "gx", "gy", "gz", None)
    return jax.shard_map(
        local,
        mesh=mesh,
        in_specs=(placed, placed, placed, P("gx", "gy", "gz"), P()),
        out_specs=placed,
        check_vma=False,
    )
```
